256 devices in a mesh: dp: 64 (over x, z, core), proto: 4 (over y).
Axes of the slice: x: 4, y: 4, z: 8, core: 2. Of those that a mesh axis runs over, the one named last changes fastest.
Arguments:
- teacher_feats: bfloat16 [8192, 2, 256], P('dp'), may hold values from -0.5 to 0.5
- student_embeddings: bfloat16 [8192, 6, 256], P('dp'), may hold values from -0.5 to 0.5
- teacher_weight: float32 [256, 32768], P('dp', 'proto'), may hold values from -0.5 to 0.5
- student_weight: float32 [256, 32768], P('dp', 'proto'), may hold values from -0.375 to 0.375
Outputs:
- weight_grad: float32 [256, 32768], P('dp', 'proto')
- teacher_new: float32 [256, 32768], P('dp', 'proto')
- feature_grad: float32 [8192, 6, 256], P('dp')
The draws below stay inside these ranges and needn't reach their ends.
All inputs are finite; a program needn't handle non-finite values.
Results may differ from the reference program's by a relative error of at most 0.00135.
The reference program's roundings to bfloat16 on the way (of `slope`) count: a program that leaves them out, or rounds other values in their place, can miss the bound.
Values may be sent and summed in bfloat16 or wider, within the bound.
No kernel may reach another device: no remote copies, remote signals or barrier semaphores. Data moves between devices by JAX's collectives and lax.ppermute only.
A program may use at most 256 MiB of HBM per device.

```python
import math
import jax
import jax.numpy as jnp
from jax import lax

BOT = 256
K = 32768
BALANCING_ROUNDS = 3
IMAGES = 8192


group_count = 8


def shared_basis(key):
    return jax.random.truncated_normal(key, -4.0, 4.0, (group_count, BOT), jnp.float32)


def image_clusters(key):
    inner = jax.random.fold_in(key, 3)
    key_first, key_second = jax.random.split(inner, 2)
    return jnp.minimum(jax.random.randint(key_first, (IMAGES,), 0, group_count), jax.random.randint(key_second, (IMAGES,), 0, group_count))


def draw_teacher_weight(key, part):
    basis = shared_basis(key)
    key = jax.random.fold_in(key, 7)
    key_group, key_noise, key_scale = jax.random.split(key, 3)
    groups = jax.random.randint(key_group, (K,), 0, group_count)
    common = 0.35 * jnp.take(basis, groups, axis=0).T
    noise = jax.random.truncated_normal(key_noise, -4.0, 4.0, (BOT, K), jnp.float32)
    spread = jnp.exp(jax.random.uniform(key_scale, (1, K), jnp.float32, math.log(0.5), math.log(2.0)))
    return jnp.clip((common + noise) * spread * BOT ** (-0.5), -0.5, 0.5)


def draw_teacher_feats(key, part):
    basis = shared_basis(key)
    cluster = image_clusters(key)
    key = jax.random.fold_in(key, 3)
    key_noise = jax.random.fold_in(key, 2)
    key_scale = jax.random.fold_in(key, 3)
    common = jnp.take(basis, cluster, axis=0)[:, None, :]
    noise = jax.random.truncated_normal(key_noise, -4.0, 4.0, (IMAGES, 2, BOT), jnp.float32)
    spread = jnp.exp(jax.random.uniform(key_scale, (IMAGES, 2, 1), jnp.float32, math.log(0.5), math.log(2.0)))
    return jnp.clip((common + noise) * spread * 0.0625, -0.5, 0.5).astype(jnp.bfloat16)


def draw_student_embeddings(key, part):
    basis = shared_basis(key)
    cluster = image_clusters(key)
    key = jax.random.fold_in(key, 11)
    key_noise, key_scale = jax.random.split(key, 2)
    position = jnp.arange(IMAGES, dtype=jnp.float32) / IMAGES
    common = jnp.take(basis, cluster, axis=0)[:, None, :]
    strength = 0.2 + 2.8 * position
    noise = jax.random.truncated_normal(key_noise, -4.0, 4.0, (IMAGES, 6, BOT), jnp.float32)
    spread = jnp.exp(jax.random.uniform(key_scale, (IMAGES, 6, 1), jnp.float32, math.log(0.5), math.log(2.0)))
    rows = common * strength[:, None, None] + noise
    return jnp.clip(rows * spread * 0.04, -0.5, 0.5).astype(jnp.bfloat16)


def shard_levels(rng, shape, cuts, low, largest):
    factor_of = 1.0
    for axis_at, shards_of in cuts:
        heights = jax.random.uniform(jax.random.fold_in(jax.random.fold_in(rng, 6), axis_at), (shards_of,), jnp.float32, low / len(cuts), largest / len(cuts))
        factor_of = factor_of * jnp.repeat(jnp.exp(heights), shape[axis_at] // shards_of).reshape((-1,) + (1,) * (len(shape) - 1 - axis_at))
    return factor_of


def normal_values(rng, dims, scale, bound, shards=(), kind=jnp.bfloat16):
    drawn = scale * jax.random.normal(rng, dims, jnp.float32)
    if shards:
        drawn = drawn * shard_levels(rng, dims, shards, -0.22, 0.18)
    return jnp.clip(drawn, -bound, bound).astype(kind)


def setup_inputs(seed: int = 0) -> dict:
    streams_of = jax.random.split(jax.random.key(seed), 5)
    return {
        "teacher_feats": draw_teacher_feats(jax.random.fold_in(streams_of[4], 71), 0),
        "student_embeddings": draw_student_embeddings(jax.random.fold_in(streams_of[4], 71), 0),
        "teacher_weight": draw_teacher_weight(jax.random.fold_in(streams_of[4], 71), 0),
        "student_weight": normal_values(streams_of[3], (BOT, K), BOT ** -0.5, 0.375, ((0, 64), (1, 4)), jnp.float32),
    }


EPS = 1e-06
TEMP_T = 0.07
TEMP_S = 0.1

def reference(teacher_feats, student_embeddings, teacher_weight, student_weight):
    col_s = jnp.sqrt(lax.optimization_barrier(jnp.sum(student_weight * student_weight, axis=0)) + EPS)
    col_t = jnp.sqrt(lax.optimization_barrier(jnp.sum(teacher_weight * teacher_weight, axis=0)) + EPS)
    proto_s = (student_weight / col_s).astype(jnp.bfloat16)
    proto_t = (teacher_weight / col_t).astype(jnp.bfloat16)
    block = math.gcd(IMAGES, 64)
    nblocks = IMAGES // block
    t_rows = teacher_feats.reshape(IMAGES * 2, BOT).astype(jnp.float32)
    t_unit = (t_rows / jnp.sqrt(lax.optimization_barrier(jnp.sum(t_rows * t_rows, axis=1, keepdims=True)) + EPS)).astype(jnp.bfloat16)
    t_blocks = t_unit.reshape(nblocks, block * 2, BOT)
    s_blocks = student_embeddings.reshape(nblocks, block * 6, BOT)

    def energy_of(rows):
        return jnp.exp(jnp.dot(rows, proto_t, preferred_element_type=jnp.float32) / TEMP_T)

    def row_scale(energy, recip):
        return 1.0 / lax.optimization_barrier(jnp.sum(energy * recip[None, :], axis=1))

    def sweep(rows, recip):
        energy = energy_of(rows)
        return lax.optimization_barrier(jnp.sum(energy * row_scale(energy, recip)[:, None], axis=0))
    recip = 1.0 / lax.optimization_barrier(jnp.sum(lax.map(lambda rows: lax.optimization_barrier(jnp.sum(energy_of(rows), axis=0)), t_blocks), axis=0))
    for round_number in range(BALANCING_ROUNDS - 1):
        current = recip
        recip = 1.0 / lax.optimization_barrier(jnp.sum(lax.map(lambda rows: sweep(rows, current), t_blocks), axis=0))
    pairing = jnp.array([[0, 1, 1, 1, 1, 1], [1, 0, 1, 1, 1, 1]], jnp.float32)
    counts = jnp.array([1, 1, 2, 2, 2, 2], jnp.float32)

    def scan_step(gradient_running, inputs):
        rows_t, rows_s = inputs
        energy = energy_of(rows_t)
        targets = (energy * recip[None, :] * row_scale(energy, recip)[:, None]).reshape(block, 2, K)
        s_rows = rows_s.astype(jnp.float32)
        s_norm = jnp.sqrt(lax.optimization_barrier(jnp.sum(s_rows * s_rows, axis=1, keepdims=True)) + EPS)
        s_float = s_rows / s_norm
        s_unit = s_float.astype(jnp.bfloat16)
        prototype_scores = (jnp.dot(s_unit, proto_s, preferred_element_type=jnp.float32) / TEMP_S).reshape(block, 6, K)
        lse = jnp.log(lax.optimization_barrier(jnp.sum(jnp.exp(prototype_scores), axis=-1)))
        prob = jnp.exp(prototype_scores - lse[..., None])
        tpart = pairing[0][None, :, None] * targets[:, 0:1, :] + pairing[1][None, :, None] * targets[:, 1:2, :]
        slope = (K / 16.0 * (counts[None, :, None] * prob - tpart)).astype(jnp.bfloat16).reshape(block * 6, K)
        gradient_running = gradient_running + lax.dot_general(s_unit, slope, (((0,), (0,)), ((), ())), preferred_element_type=jnp.float32)
        unit_grad = lax.dot_general(slope, proto_s, (((1,), (1,)), ((), ())), preferred_element_type=jnp.float32)
        fgrad = (unit_grad - s_float * lax.optimization_barrier(jnp.sum(s_float * unit_grad, axis=1, keepdims=True))) / s_norm
        return (gradient_running, fgrad)
    init = jnp.zeros((BOT, K), jnp.float32)
    proto_grad, fgrads = lax.scan(scan_step, init, (t_blocks, s_blocks))
    column_dot = lax.optimization_barrier(jnp.sum(proto_s.astype(jnp.float32) * proto_grad, axis=0))
    weight_grad = (proto_grad - proto_s.astype(jnp.float32) * column_dot) / col_s
    teacher_new = 0.994 * teacher_weight + 0.006 * (student_weight - 0.5 * weight_grad)
    feature_grad = fgrads.reshape(IMAGES, 6, BOT)
    return (weight_grad, teacher_new, feature_grad)
```

```python
import jax
import jax.numpy as jnp
from jax import lax
from jax.experimental import pallas as pl
from jax.experimental.pallas import tpu as pltpu
from jax.sharding import Mesh, PartitionSpec as P

BALANCING_ROUNDS = 3
EPS = 1e-06
TEMP_T = 0.07
TEMP_S = 0.1
CROPS = 6
COUNTS = (1.0, 1.0, 2.0, 2.0, 2.0, 2.0)
NX, NZ, NC, NY = 4, 8, 2, 4
DP = ("x", "z", "core")
XY = ("x", "proto")


def spread(v, axes, n):
    return lax.all_to_all(jnp.broadcast_to(v, (n,) + v.shape), axes, 0, 0)


def other_core(v):
    return lax.ppermute(v, "core", [(0, 1), (1, 0)])


def shifted(v, axis, n, k):
    return lax.ppermute(v, axis, [(i, (i + k) % n) for i in range(n)])


def along(v, axis, n):
    me = lax.axis_index(axis)
    out = jnp.zeros((n,) + v.shape, v.dtype)
    for k in range(n):
        part = v if k == 0 else shifted(v, axis, n, k)
        out = lax.dynamic_update_index_in_dim(out, part, (me - k) % n, 0)
    return out


def slope_kernel(
    factor, images, tile, place_ref, s_ref, ps_ref, e_ref, r_ref, c_ref, a_ref, ug_ref, pg_ref, slope_ref, total_ref
):
    width = ps_ref.shape[1]

    @pl.when(pl.program_id(0) == 0)
    def _():
        total_ref[...] = jnp.zeros_like(total_ref)

    def columns(j, _):
        at = pl.ds(pl.multiple_of(j * tile, tile), tile)
        recip = r_ref[:, at] * factor
        t0 = e_ref[0, :images, at] * recip * c_ref[0, :images, :]
        t1 = e_ref[0, images:, at] * recip * c_ref[0, images:, :]
        both = t0 + t1
        for crop in range(CROPS):
            rows = slice(crop * images, (crop + 1) * images)
            scores = jnp.dot(s_ref[0, rows, :], ps_ref[:, at], preferred_element_type=jnp.float32)
            part = a_ref[0, rows, :] * jnp.exp(scores * (1.0 / TEMP_S))
            minus = t1 if crop == 0 else t0 if crop == 1 else both
            slope_ref[rows, at] = (part - minus).astype(jnp.bfloat16)
        total_ref[:, at] += lax.dot_general(
            s_ref[0], slope_ref[:, at], (((0,), (0,)), ((), ())), preferred_element_type=jnp.float32
        )
        return 0

    lax.fori_loop(0, width // tile, columns, 0)
    unit = lax.dot_general(
        slope_ref[...], ps_ref[...], (((1,), (1,)), ((), ())), preferred_element_type=jnp.float32
    )
    part = images // NY
    for crop in range(CROPS):
        for y in range(NY):
            ug_ref[0, y, crop * part : (crop + 1) * part, :] = unit[crop * images + y * part :][:part]

    @pl.when(pl.program_id(0) == pl.num_programs(0) - 1)
    def _():
        sub = pg_ref.shape[3]
        for side in range(NC):
            for k in range(NZ):
                z = lax.rem(place_ref[0] + k, NZ)
                c = lax.rem(place_ref[1] + side, NC)
                pg_ref[side, k] = total_ref[:, pl.ds(pl.multiple_of((c * NZ + z) * sub, sub), sub)]


def slopes(place, s_unit, proto_s, energy, recip, scales, amount, factor):
    groups, rows, bottleneck = s_unit.shape
    t_rows = energy.shape[1]
    width = proto_s.shape[1]
    images = rows // CROPS
    sub = width // (NC * NZ)
    return pl.pallas_call(
        lambda *refs: slope_kernel(factor, images, 512, *refs),
        grid=(groups,),
        in_specs=[
            pl.BlockSpec(memory_space=pltpu.SMEM),
            pl.BlockSpec((1, rows, bottleneck), lambda g: (g, 0, 0)),
            pl.BlockSpec((bottleneck, width), lambda g: (0, 0)),
            pl.BlockSpec((1, t_rows, width), lambda g: (g, 0, 0)),
            pl.BlockSpec((1, width), lambda g: (0, 0)),
            pl.BlockSpec((1, t_rows, 1), lambda g: (g, 0, 0)),
            pl.BlockSpec((1, rows, 1), lambda g: (g, 0, 0)),
        ],
        out_specs=[
            pl.BlockSpec((1, NY, rows // NY, bottleneck), lambda g: (g, 0, 0, 0)),
            pl.BlockSpec((NC, NZ, bottleneck, sub), lambda g: (0, 0, 0, 0)),
        ],
        out_shape=[
            jax.ShapeDtypeStruct((groups, NY, rows // NY, bottleneck), jnp.float32),
            jax.ShapeDtypeStruct((NC, NZ, bottleneck, sub), jnp.float32),
        ],
        scratch_shapes=[pltpu.VMEM((rows, width), jnp.bfloat16), pltpu.VMEM((bottleneck, width), jnp.float32)],
        compiler_params=pltpu.CompilerParams(vmem_limit_bytes=48 * 1024 * 1024),
        cost_estimate=pl.CostEstimate(
            flops=6 * groups * rows * bottleneck * width,
            bytes_accessed=4 * groups * (t_rows * width + rows * bottleneck),
            transcendentals=groups * rows * width,
        ),
    )(place, s_unit, proto_s, energy, recip, scales, amount)


def local(teacher_feats, student_embeddings, teacher_weight, student_weight):
    images, _, bottleneck = teacher_feats.shape
    rows_here, wide = student_weight.shape
    sub = wide // (NX * NZ * NC)
    width = wide // NX
    total_k = wide * NY
    s_rows = images * CROPS
    t_rows = images * 2

    shards = jnp.stack([teacher_weight, student_weight]).reshape(2 * rows_here, NX * NZ * NC, sub)
    moved = lax.all_to_all(shards.transpose(1, 0, 2), DP, 0, 0)
    moved = moved.reshape(NX * NZ * NC, 2, rows_here, sub)
    cols_t = moved[:, 0].reshape(bottleneck, sub)
    cols_s = moved[:, 1].reshape(bottleneck, sub)
    col_t = jnp.sqrt(jnp.sum(cols_t * cols_t, axis=0) + EPS)
    col_s = jnp.sqrt(jnp.sum(cols_s * cols_s, axis=0) + EPS)
    mine_t = (cols_t / col_t).astype(jnp.bfloat16)
    mine_s = (cols_s / col_s).astype(jnp.bfloat16)

    place = jnp.stack([lax.axis_index("z"), lax.axis_index("core")]).astype(jnp.int32)

    def gather_columns(mine):
        own = spread(mine, "z", NZ)
        other = other_core(own)
        first = lax.axis_index("core") == 0
        both = jnp.stack([jnp.where(first, own, other), jnp.where(first, other, own)])
        return both.transpose(2, 0, 1, 3).reshape(bottleneck, width)

    t_float = teacher_feats.transpose(1, 0, 2).reshape(t_rows, bottleneck).astype(jnp.float32)
    t_unit = (t_float / jnp.sqrt(jnp.sum(t_float * t_float, axis=1, keepdims=True) + EPS)).astype(jnp.bfloat16)
    s_raw = student_embeddings.transpose(1, 0, 2).reshape(s_rows, bottleneck).astype(jnp.float32)
    s_norm = jnp.sqrt(jnp.sum(s_raw * s_raw, axis=1, keepdims=True) + EPS)
    s_float = s_raw / s_norm
    s_unit = s_float.astype(jnp.bfloat16)
    t_all = along(t_unit, "x", NX)
    s_all = lax.all_gather(s_unit, "x")

    proto_t = gather_columns(mine_t)
    energy = jnp.exp(
        jnp.dot(t_all.reshape(NX * t_rows, bottleneck), proto_t, preferred_element_type=jnp.float32) / TEMP_T
    )
    proto_s = lax.all_gather(mine_s, ("core", "z")).transpose(1, 0, 2).reshape(bottleneck, width)
    scores = jnp.dot(s_all.reshape(NX * s_rows, bottleneck), proto_s, preferred_element_type=jnp.float32)
    expsum = jnp.sum(jnp.exp(scores / TEMP_S), axis=1)

    scales = None
    for round_number in range(BALANCING_ROUNDS):
        weighted = energy if scales is None else energy * scales[:, None]
        over_rows = jnp.sum(weighted, axis=0)
        recip = 1.0 / jnp.sum(spread(over_rows, ("z", "core"), NZ * NC), axis=0)
        over_cols = jnp.sum(energy * recip[None, :], axis=1)
        if round_number == BALANCING_ROUNDS - 1:
            over_cols = jnp.concatenate([over_cols, expsum])
        summed = jnp.sum(spread(over_cols, XY, NX * NY), axis=0)
        scales = 1.0 / summed[: NX * t_rows]
    expsum = summed[NX * t_rows :].reshape(NX, CROPS, images)

    factor = total_k / 16.0
    amount = factor * jnp.array(COUNTS, jnp.float32)[None, :, None] / expsum
    unit_part, proto_part = slopes(
        place,
        s_all,
        proto_s,
        energy.reshape(NX, t_rows, width),
        recip.reshape(1, width),
        scales.reshape(NX, t_rows, 1),
        amount.reshape(NX, s_rows, 1),
        factor,
    )

    half = (proto_part[0] + other_core(proto_part[1])) * (1.0 / 512.0)
    proto_grad = half[0]
    for k in range(1, NZ):
        proto_grad = proto_grad + shifted(half[k].astype(jnp.float16), "z", NZ, k).astype(jnp.float32)
    proto_grad = proto_grad * 512.0
    proto_float = mine_s.astype(jnp.float32)
    column_dot = jnp.sum(proto_float * proto_grad, axis=0)
    grad_cols = (proto_grad - proto_float * column_dot) / col_s
    grad_rows = lax.all_to_all(grad_cols.reshape(NX * NZ * NC, rows_here, sub), DP, 0, 0)
    weight_grad = grad_rows.transpose(1, 0, 2).reshape(rows_here, wide)
    teacher_new = 0.994 * teacher_weight + 0.006 * (student_weight - 0.5 * weight_grad)

    quarter = images // NY
    sent = (unit_part.reshape(NX * NY, CROPS * quarter, bottleneck) * 4.0).astype(jnp.float16)
    unit_grad = jnp.sum(lax.all_to_all(sent, XY, 0, 0).astype(jnp.float32), axis=0) * 0.25
    unit_grad = unit_grad.reshape(CROPS, quarter, bottleneck)
    first = lax.axis_index("proto") * quarter
    part_float = lax.dynamic_slice_in_dim(s_float.reshape(CROPS, images, bottleneck), first, quarter, 1)
    part_norm = lax.dynamic_slice_in_dim(s_norm.reshape(CROPS, images, 1), first, quarter, 1)
    fgrad = (unit_grad - part_float * jnp.sum(part_float * unit_grad, axis=2, keepdims=True)) / part_norm
    feature_grad = along(fgrad.transpose(1, 0, 2), "proto", NY).reshape(images, CROPS, bottleneck)
    return weight_grad, teacher_new, feature_grad


def solution(mesh):
    fine = Mesh(mesh.devices.reshape(NX, NZ, NC, NY), ("x", "z", "core", "proto"))
    in_specs = (P(DP, None, None), P(DP, None, None), P(DP, "proto"), P(DP, "proto"))
    out_specs = (P(DP, "proto"), P(DP, "proto"), P(DP, None, None))
    return jax.shard_map(local, mesh=fine, in_specs=in_specs, out_specs=out_specs, check_vma=False)
```

```python
import functools

import jax
import jax.numpy as jnp
from jax import lax
from jax.experimental import pallas as pl
from jax.experimental.pallas import tpu as pltpu
from jax.sharding import Mesh, PartitionSpec as P

BALANCING_ROUNDS = 3
EPS = 1e-06
TEMP_T = 0.07
TEMP_S = 0.1
CROPS = 6
NX, NZ, NC, NY = 4, 8, 2, 4
DP = ("x", "z", "core")
XY = ("x", "proto")
ZC = ("z", "core")
LANES = 128
BY_BITS = [b4 * 4 + b2 * 2 + b1 for b2 in range(2) for b1 in range(2) for b4 in range(2)]
LOG2E = 1.4426950408889634
MIB = 1024 * 1024
VMEM = pl.BlockSpec(memory_space=pltpu.VMEM)
SMEM = pl.BlockSpec(memory_space=pltpu.SMEM)
HBM = pl.BlockSpec(memory_space=pltpu.HBM)


def swap(v, axes):
    return lax.all_to_all(v, axes, 0, 0)


def spread(v, axes, n):
    return swap(jnp.broadcast_to(v, (n,) + v.shape), axes)


def other_core(v):
    return lax.ppermute(v, "core", [(0, 1), (1, 0)])


def shifted(v, axis, n, k):
    return lax.ppermute(v, axis, [(i, (i + k) % n) for i in range(n)])


def along(v, axis, n):
    me = lax.axis_index(axis)
    out = jnp.zeros((n,) + v.shape, v.dtype)
    for k in range(n):
        part = v if k == 0 else shifted(v, axis, n, k)
        out = lax.dynamic_update_index_in_dim(out, part, (me - k) % n, 0)
    return out


def exchanged(v, axis, n, step):
    return v, lax.ppermute(v, axis, [(i, i ^ step) for i in range(n)])


def merged(pair, axis, step):
    own, got = pair
    high = (lax.axis_index(axis) // step) % 2 == 1
    return jnp.concatenate([jnp.where(high, got, own), jnp.where(high, own, got)])


def whole(*shape):
    return pl.BlockSpec(shape, lambda *at: (0,) * len(shape))


def call(kernel, out_shape, in_specs, scratch=(), out_specs=None, grid=(), limit=8, flops=0, moved=0, exps=0):
    return pl.pallas_call(
        kernel,
        grid=grid,
        out_shape=out_shape,
        in_specs=in_specs,
        out_specs=out_specs or [VMEM] * len(out_shape),
        scratch_shapes=list(scratch),
        compiler_params=pltpu.CompilerParams(vmem_limit_bytes=limit * MIB),
        cost_estimate=pl.CostEstimate(flops=flops, bytes_accessed=moved, transcendentals=exps),
    )


def down(row):
    return jnp.transpose(jnp.broadcast_to(row, (LANES, LANES)))


def fold(v, rows):
    return jnp.sum(v.reshape(v.shape[0] // rows, rows, v.shape[1]), axis=0)


def join_columns(place_ref, own_ref, other_ref, out_ref, order=range(NZ)):
    for side, ref in enumerate((own_ref, other_ref)):
        half = lax.rem(place_ref[1] + side, NC) * NZ
        for i, z in enumerate(order):
            out_ref[:, pl.ds(pl.multiple_of((half + z) * LANES, LANES), LANES)] = ref[i]


def to_all(acc, out_ref, n):
    total = jnp.sum(acc, axis=0, keepdims=True)
    count = total.shape[1] // LANES
    lines = jnp.concatenate([total[:, i * LANES : (i + 1) * LANES] for i in range(count)], axis=0)
    for p in range(n):
        out_ref[p, :count] = lines


def energy_kernel(place_ref, norm_ref, t_ref, own_ref, other_ref, e_ref, out_ref, proto_ref, acc_ref, held_ref, sem_ref):
    join_columns(place_ref, own_ref, other_ref, proto_ref)
    width = e_ref.shape[1]
    tile = 256

    def copy(j):
        at = pl.ds(pl.multiple_of(j * tile, tile), tile)
        return pltpu.make_async_copy(held_ref.at[:, at], e_ref.at[:, at], sem_ref.at[j])

    def columns(j, _):
        at = pl.ds(pl.multiple_of(j * tile, tile), tile)
        dots = jnp.dot(t_ref[...], proto_ref[:, at], preferred_element_type=jnp.float32)
        energy = jnp.exp(dots * (1.0 / TEMP_T))
        held_ref[:, at] = energy
        acc_ref[:, at] = fold(energy, 8)
        copy(j).start()
        return 0

    lax.fori_loop(0, width // tile, columns, 0)
    to_all(acc_ref[...], out_ref, out_ref.shape[0])
    for p in range(out_ref.shape[0]):
        out_ref[p, width // LANES : width // LANES + 1] = norm_ref[...]
    for j in range(width // tile):
        copy(j).wait()


def fetch(e_ref, held_ref, sem_ref):
    blocks = e_ref.shape[0] // LANES

    def copy(b):
        at = pl.ds(pl.multiple_of(b * LANES, LANES), LANES)
        return pltpu.make_async_copy(e_ref.at[at], held_ref.at[at], sem_ref.at[b])

    for b in range(blocks):
        copy(b).start()
    return blocks, lambda b: copy(b).wait()


def by_row_kernel(got_ref, e_ref, *refs):
    more = refs[:-5]
    recip_ref, out_ref, lines_ref, held_ref, sem_ref = refs[-5:]
    blocks, wait = fetch(e_ref, held_ref, sem_ref)
    width = e_ref.shape[1]
    count = width // LANES
    recip = 1.0 / jnp.sum(got_ref[:, :count], axis=0)
    for i in range(count):
        recip_ref[:, i * LANES : (i + 1) * LANES] = recip[i : i + 1, :]

    def block(b, _):
        wait(b)
        at = pl.ds(pl.multiple_of(b * LANES, LANES), LANES)
        acc = jnp.zeros((LANES, LANES), jnp.float32)
        for j in range(width // LANES):
            lanes = slice(j * LANES, (j + 1) * LANES)
            acc += held_ref[at, lanes] * recip_ref[:, lanes]
        lines_ref[pl.ds(b, 1), :] = jnp.sum(jnp.transpose(acc), axis=0, keepdims=True)
        return 0

    lax.fori_loop(0, blocks, block, 0)
    for p in range(out_ref.shape[0]):
        out_ref[p, :8] = lines_ref[...]
        at = 8
        for ref in more:
            out_ref[p, at : at + ref.shape[0]] = ref[...]
            at += ref.shape[0]


def by_column_kernel(got_ref, e_ref, out_ref, lines_ref, acc_ref, held_ref, sem_ref):
    blocks, wait = fetch(e_ref, held_ref, sem_ref)
    width = e_ref.shape[1]
    lines_ref[...] = 1.0 / jnp.sum(got_ref[...], axis=0)
    acc_ref[...] = jnp.zeros_like(acc_ref)

    def block(b, _):
        wait(b)
        at = pl.ds(pl.multiple_of(b * LANES, LANES), LANES)
        scale = down(lines_ref[pl.ds(b, 1), :])
        for j in range(width // LANES):
            lanes = slice(j * LANES, (j + 1) * LANES)
            acc_ref[:, lanes] += fold(held_ref[at, lanes] * scale, 8)
        return 0

    lax.fori_loop(0, blocks, block, 0)
    to_all(acc_ref[...], out_ref, out_ref.shape[0])


def student_sums(s_ref, proto_ref, sums_ref):
    width = proto_ref.shape[1]

    def block(b, _):
        at = pl.ds(pl.multiple_of(b * 2 * LANES, 2 * LANES), 2 * LANES)
        acc = jnp.zeros((2 * LANES, LANES), jnp.float32)
        for j in range(width // 256):
            dots = jnp.dot(
                s_ref[at, :], proto_ref[:, j * 256 : (j + 1) * 256], preferred_element_type=jnp.float32
            )
            powers = jnp.exp2(dots * (LOG2E / TEMP_S))
            acc += powers[:, :LANES] + powers[:, LANES:]
        for i in range(2):
            part = acc[i * LANES : (i + 1) * LANES]
            sums_ref[pl.ds(b * 2 + i, 1), :] = jnp.sum(jnp.transpose(part), axis=0, keepdims=True)
        return 0

    lax.fori_loop(0, s_ref.shape[0] // (2 * LANES), block, 0)


def student_kernel(place_ref, s_ref, own_ref, other_ref, proto_ref, sums_ref):
    join_columns(place_ref, own_ref, other_ref, proto_ref, BY_BITS)
    student_sums(s_ref, proto_ref, sums_ref)


def slope_kernel(
    factor, place_ref, got_ref, recip_ref, s_ref, st_ref, ps_ref, psp_ref, e_ref,
    ug_ref, keep_ref, give_ref, slope_ref, total_ref, lines_ref, down_ref,
):
    rows = st_ref.shape[2]
    width = ps_ref.shape[1]
    images = rows // CROPS
    tile = 1024
    g = pl.program_id(0)
    groups = pl.num_programs(0)

    @pl.when(g == 0)
    def _():
        lines_ref[...] = factor / jnp.sum(got_ref[...], axis=0)
        total_ref[...] = jnp.zeros_like(total_ref)

    for i in range(2):
        down_ref[i] = down(lines_ref[pl.ds(g * 2 + i, 1), :])
    for crop in range(CROPS):
        line = down(lines_ref[pl.ds(groups * 2 + g * CROPS + crop, 1), :])
        down_ref[2 + crop] = line if crop < 2 else 2.0 * line

    def columns(j, _):
        at = pl.ds(pl.multiple_of(j * tile, tile), tile)
        wide = lambda i: jnp.concatenate([down_ref[i]] * (tile // LANES), axis=1)
        recip = recip_ref[:, at]
        t0 = e_ref[:images, at] * recip * wide(0)
        t1 = e_ref[images:, at] * recip * wide(1)
        both = t0 + t1
        scores = jnp.dot(s_ref[0], ps_ref[:, at], preferred_element_type=jnp.float32)
        for crop in range(CROPS):
            lines = slice(crop * images, (crop + 1) * images)
            part = wide(2 + crop) * jnp.exp2(scores[lines] * (LOG2E / TEMP_S))
            minus = t1 if crop == 0 else t0 if crop == 1 else both
            slope_ref[lines, at] = (part - minus).astype(jnp.bfloat16)
        return 0

    lax.fori_loop(0, width // tile, columns, 0)
    total_ref[...] += jnp.dot(st_ref[0], slope_ref[...], preferred_element_type=jnp.float32)
    unit = lax.dot_general(
        slope_ref[...], ps_ref[...], (((1,), (1,)), ((), ())), preferred_element_type=jnp.float32
    )
    part = images // NY
    for crop in range(CROPS):
        for y in range(NY):
            ug_ref[0, y, crop * part : (crop + 1) * part, :] = unit[crop * images + y * part :][:part]

    @pl.when(g == groups - 1)
    def _():
        blocks = width // LANES
        part = total_ref.shape[0] // (NC * NZ)
        size = blocks * part
        for b in range(blocks):
            lanes = slice(b * LANES, (b + 1) * LANES)
            dot = jnp.sum(psp_ref[:, lanes].astype(jnp.float32) * total_ref[:, lanes], axis=0, keepdims=True)
            keep_ref[NZ * size + b : NZ * size + b + 1, :] = dot
            give_ref[NZ * size + b : NZ * size + b + 1, :] = dot
        for side, ref in enumerate((keep_ref, give_ref)):
            half = lax.rem(place_ref[1] + side, NC) * NZ
            for k in range(NZ):
                z = lax.rem(place_ref[0] + k, NZ)
                lines = total_ref[pl.ds(pl.multiple_of((half + z) * part, part), part), :]
                for b in range(blocks):
                    at = k * size + b * part
                    ref[at : at + part, :] = lines[:, b * LANES : (b + 1) * LANES]


def local(teacher_feats, student_embeddings, teacher_weight, student_weight):
    images, _, bottleneck = teacher_feats.shape
    rows_here, wide = student_weight.shape
    sub = wide // (NX * NZ * NC)
    width = wide // NX
    total_k = wide * NY
    s_rows = images * CROPS
    t_rows = images * 2
    f32, bf16 = jnp.float32, jnp.bfloat16
    shape = jax.ShapeDtypeStruct
    place = jnp.stack([lax.axis_index("z"), lax.axis_index("core")]).astype(jnp.int32)
    exact = NX * t_rows * width

    t_float = teacher_feats.transpose(1, 0, 2).reshape(t_rows, bottleneck).astype(f32)
    t_unit = (t_float / jnp.sqrt(jnp.sum(t_float * t_float, axis=1, keepdims=True) + EPS)).astype(bf16)

    shards = jnp.stack([teacher_weight, student_weight]).reshape(2 * rows_here, NX * NZ * NC, sub)
    moved, t_unit = lax.optimization_barrier((swap(shards.transpose(1, 0, 2), DP), t_unit))
    t_all = along(t_unit, "x", NX).reshape(NX * t_rows, bottleneck)
    moved = moved.reshape(NX * NZ * NC, 2, rows_here, sub)
    cols_t = moved[:, 0].reshape(bottleneck, sub)
    cols_s = moved[:, 1].reshape(bottleneck, sub)
    col_t = jnp.sqrt(jnp.sum(cols_t * cols_t, axis=0) + EPS)
    col_s = jnp.sqrt(jnp.sum(cols_s * cols_s, axis=0) + EPS)
    mine_t = (cols_t / col_t).astype(bf16)
    mine_s = (cols_s / col_s).astype(bf16)

    s_raw = student_embeddings.transpose(1, 0, 2).reshape(s_rows, bottleneck).astype(f32)
    s_norm = jnp.sqrt(jnp.sum(s_raw * s_raw, axis=1, keepdims=True) + EPS)
    s_float = s_raw / s_norm
    s_unit, mine_t, mine_s = lax.optimization_barrier((s_float.astype(bf16), mine_t, mine_s))
    pair = exchanged(mine_s[None], "z", NZ, 4)
    s_pair = exchanged(s_unit[None], "x", NX, 1)
    own_t = spread(mine_t, "z", NZ)
    energy, to_devices = call(
        energy_kernel,
        [pltpu.HBM((NX * t_rows, width), f32), shape((NZ * NC, width // LANES + 8, LANES), f32)],
        [SMEM, VMEM, VMEM, VMEM, VMEM],
        [
            pltpu.VMEM((bottleneck, width), bf16),
            pltpu.VMEM((8, width), f32),
            pltpu.VMEM((NX * t_rows, width), f32),
            pltpu.SemaphoreType.DMA((width // 256,)),
        ],
        [HBM, VMEM],
        limit=24,
        flops=2 * exact * bottleneck,
        exps=exact,
    )(place, col_s.reshape(1, sub), t_all, own_t, other_core(own_t))

    energy = pltpu.with_memory_space_constraint(energy, pltpu.HBM)
    blocks = NX * t_rows // LANES
    held = [pltpu.VMEM((NX * t_rows, width), f32), pltpu.SemaphoreType.DMA((blocks,))]
    quarter = images // NY
    first = lax.axis_index("proto") * quarter
    part_float = lax.dynamic_slice_in_dim(s_float.reshape(CROPS, images, bottleneck), first, quarter, 1)
    part_norm = lax.dynamic_slice_in_dim(s_norm.reshape(CROPS, images, 1), first, quarter, 1)
    part_float, part_norm, to_devices = lax.optimization_barrier((part_float, part_norm, to_devices))

    def by_row(got, *more):
        lines = 8 + sum(m.shape[0] for m in more)
        return call(
            by_row_kernel,
            [shape((1, width), f32), shape((NX * NY, lines, LANES), f32)],
            [VMEM, HBM] + [VMEM] * len(more),
            [pltpu.VMEM((8, LANES), f32)] + held,
            limit=12,
            flops=2 * exact,
            moved=4 * exact,
        )(got, energy, *more)

    def by_column(got):
        (to_devices,) = call(
            by_column_kernel,
            [shape((NZ * NC, width // LANES, LANES), f32)],
            [VMEM, HBM],
            [pltpu.VMEM((8, LANES), f32), pltpu.VMEM((8, width), f32)] + held,
            limit=12,
            flops=2 * exact,
            moved=4 * exact,
        )(got, energy)
        return to_devices

    half_rows = NX * s_rows // 2
    student = dict(limit=58, flops=exact * 3 * bottleneck, exps=exact * 3 // 2)

    to_devices, own_s = lax.optimization_barrier((to_devices, merged(pair, "z", 4)))
    got = swap(to_devices, ZC)
    pair = exchanged(own_s, "z", NZ, 1)
    col_s = got[:, width // LANES].reshape(NZ, NC, LANES).transpose(1, 0, 2).reshape(NZ * NC, 1, LANES)
    _, to_devices = by_row(got)
    to_devices, own_s, s_all = lax.optimization_barrier((to_devices, merged(pair, "z", 1), merged(s_pair, "x", 1)))
    got = swap(to_devices, XY)
    pair = exchanged(own_s, "z", NZ, 2)
    to_devices = by_column(got)

    to_devices, own_s, s_all = lax.optimization_barrier((to_devices, merged(pair, "z", 2), s_all))
    got = swap(to_devices, ZC)
    other_s = other_core(own_s)
    s_pair = exchanged(s_all, "x", NX, 2)
    _, to_devices = by_row(got)
    to_devices, other_s, s_pair = lax.optimization_barrier((to_devices, other_s, s_pair))
    got = swap(to_devices, XY)
    s_all = merged(s_pair, "x", 2)
    s_halves = s_all.reshape(2, half_rows, bottleneck)
    proto_s, first_sums = call(
        student_kernel,
        [shape((bottleneck, width), bf16), shape((half_rows // LANES, LANES), f32)],
        [SMEM, VMEM, VMEM, VMEM],
        **student,
    )(place, s_halves[0], own_s, other_s)
    to_devices = by_column(got)

    to_devices, proto_s, s_all, first_sums = lax.optimization_barrier((to_devices, proto_s, s_all, first_sums))
    got = swap(to_devices, ZC)
    (last_sums,) = call(
        student_sums, [shape((half_rows // LANES, LANES), f32)], [VMEM, VMEM], **student
    )(s_all.reshape(2, half_rows, bottleneck)[1], proto_s)
    recip, to_devices = by_row(got, first_sums, last_sums)
    to_devices, proto_s, s_all = lax.optimization_barrier((to_devices, proto_s, s_all))
    got = swap(to_devices, XY)

    order = jnp.arange(bottleneck).reshape(NX, NZ, NC, rows_here).transpose(2, 1, 0, 3).reshape(-1)
    ordered = (order[:, None] == jnp.arange(bottleneck)[None, :]).astype(bf16)
    proto_o = jnp.dot(ordered, proto_s, preferred_element_type=f32).astype(bf16)
    s_o = jnp.einsum("pb,grb->gpr", ordered, s_all, preferred_element_type=f32).astype(bf16)
    size = bottleneck * width // (NC * NZ * LANES)
    unit_part, keep, give = call(
        functools.partial(slope_kernel, total_k / 16.0),
        [pltpu.VMEM((NX, NY, s_rows // NY, bottleneck), f32)] + [pltpu.HBM((NZ * size + width // LANES, LANES), f32)] * NC,
        [
            SMEM,
            whole(NX * NY, NX * (2 + CROPS), LANES),
            whole(1, width),
            pl.BlockSpec((1, s_rows, bottleneck), lambda g: (g, 0, 0)),
            pl.BlockSpec((1, bottleneck, s_rows), lambda g: (g, 0, 0)),
            whole(bottleneck, width),
            whole(bottleneck, width),
            pl.BlockSpec((t_rows, width), lambda g: (g, 0)),
        ],
        [
            pltpu.VMEM((s_rows, width), bf16),
            pltpu.VMEM((bottleneck, width), f32),
            pltpu.VMEM((NX * (2 + CROPS), LANES), f32),
            pltpu.VMEM((2 + CROPS, LANES, LANES), f32),
        ],
        [
            pl.BlockSpec((1, NY, s_rows // NY, bottleneck), lambda g: (g, 0, 0, 0)),
            whole(NZ * size + width // LANES, LANES),
            whole(NZ * size + width // LANES, LANES),
        ],
        (NX,),
        limit=40,
        flops=6 * exact * 3 * bottleneck,
        moved=4 * exact,
        exps=exact * 3,
    )(
        place,
        pltpu.with_memory_space_constraint(got, pltpu.HBM),
        recip,
        *(pltpu.with_memory_space_constraint(v, pltpu.HBM) for v in (s_all, s_o, proto_s, proto_o)),
        energy,
    )

    half = (keep + other_core(give)) * (1.0 / 512.0)
    dots = half[NZ * size :]
    high = lax.reduce_precision(dots, 5, 10)
    ends = [high.astype(jnp.float16), ((dots - high) * 1024.0).astype(jnp.float16)]
    proto_grad = half[:size]
    for k in range(1, NZ):
        sent = jnp.concatenate([half[k * size : (k + 1) * size].astype(jnp.float16)] + ends)
        came = shifted(sent, "z", NZ, k).astype(f32)
        proto_grad = proto_grad + came[:size]
        dots = dots + (came[size : size + NZ * NC] + came[size + NZ * NC :] * (1.0 / 1024.0))
    lines = bottleneck // (NC * NZ)
    proto_grad = proto_grad.reshape(NC * NZ, lines, LANES) * 512.0
    column_dot = dots.reshape(NC * NZ, 1, LANES) * 512.0
    at = (lax.axis_index("core") * NZ + lax.axis_index("z")) * lines
    proto_float = lax.dynamic_slice_in_dim(proto_o, at, lines, 0).astype(f32)
    proto_float = proto_float.reshape(lines, NC * NZ, LANES).transpose(1, 0, 2)
    grad_lines = (proto_grad - proto_float * column_dot) / col_s

    sent = (unit_part.reshape(NX * NY, CROPS * quarter, bottleneck) * 4.0).astype(jnp.float16)
    unit_grad = jnp.sum(swap(sent, XY).astype(f32), axis=0) * 0.25
    unit_grad = unit_grad.reshape(CROPS, quarter, bottleneck)
    fgrad = (unit_grad - part_float * jnp.sum(part_float * unit_grad, axis=2, keepdims=True)) / part_norm

    grad_lines, fgrad = lax.optimization_barrier((grad_lines, fgrad))
    feature_grad = along(fgrad.transpose(1, 0, 2), "proto", NY).reshape(images, CROPS, bottleneck)
    grad_lines = grad_lines.reshape(NC * NZ, NX, rows_here, LANES).transpose(1, 0, 2, 3)
    grad_rows = swap(grad_lines, "x").reshape(NX, NC, NZ, rows_here, LANES)
    weight_grad = grad_rows.transpose(3, 0, 2, 1, 4).reshape(rows_here, wide)
    teacher_new = 0.994 * teacher_weight + 0.006 * (student_weight - 0.5 * weight_grad)
    return weight_grad, teacher_new, feature_grad


def solution(mesh):
    fine = Mesh(mesh.devices.reshape(NX, NZ, NC, NY), ("x", "z", "core", "proto"))
    in_specs = (P(DP, None, None), P(DP, None, None), P(DP, "proto"), P(DP, "proto"))
    out_specs = (P(DP, "proto"), P(DP, "proto"), P(DP, None, None))
    return jax.shard_map(local, mesh=fine, in_specs=in_specs, out_specs=out_specs, check_vma=False)
```

```python
import functools

import jax
import jax.numpy as jnp
from jax import lax
from jax.experimental import pallas as pl
from jax.experimental.pallas import tpu as pltpu
from jax.sharding import Mesh, PartitionSpec as P

BALANCING_ROUNDS = 3
EPS = 1e-06
TEMP_T = 0.07
TEMP_S = 0.1
CROPS = 6
NX, NZ, NC, NY = 4, 8, 2, 4
DP = ("x", "z", "core")
XY = ("x", "proto")
ZC = ("z", "core")
LANES = 128
BY_BITS = [b4 * 4 + b2 * 2 + b1 for b2 in range(2) for b1 in range(2) for b4 in range(2)]
LOG2E = 1.4426950408889634
MIB = 1024 * 1024
VMEM = pl.BlockSpec(memory_space=pltpu.VMEM)
SMEM = pl.BlockSpec(memory_space=pltpu.SMEM)
HBM = pl.BlockSpec(memory_space=pltpu.HBM)


def swap(v, axes):
    return lax.all_to_all(v, axes, 0, 0)


def spread(v, axes, n):
    return swap(jnp.broadcast_to(v, (n,) + v.shape), axes)


def other_core(v):
    return lax.ppermute(v, "core", [(0, 1), (1, 0)])


def shifted(v, axis, n, k):
    return lax.ppermute(v, axis, [(i, (i + k) % n) for i in range(n)])


def along(v, axis, n):
    me = lax.axis_index(axis)
    out = jnp.zeros((n,) + v.shape, v.dtype)
    for k in range(n):
        part = v if k == 0 else shifted(v, axis, n, k)
        out = lax.dynamic_update_index_in_dim(out, part, (me - k) % n, 0)
    return out


def exchanged(v, axis, n, step):
    return v, lax.ppermute(v, axis, [(i, i ^ step) for i in range(n)])


def merged(pair, axis, step):
    own, got = pair
    high = (lax.axis_index(axis) // step) % 2 == 1
    return jnp.concatenate([jnp.where(high, got, own), jnp.where(high, own, got)])


def whole(*shape):
    return pl.BlockSpec(shape, lambda *at: (0,) * len(shape))


def call(kernel, out_shape, in_specs, scratch=(), out_specs=None, grid=(), limit=8, flops=0, moved=0, exps=0):
    return pl.pallas_call(
        kernel,
        grid=grid,
        out_shape=out_shape,
        in_specs=in_specs,
        out_specs=out_specs or [VMEM] * len(out_shape),
        scratch_shapes=list(scratch),
        compiler_params=pltpu.CompilerParams(vmem_limit_bytes=limit * MIB),
        cost_estimate=pl.CostEstimate(flops=flops, bytes_accessed=moved, transcendentals=exps),
    )


def down(row):
    return jnp.transpose(jnp.broadcast_to(row, (LANES, LANES)))


def fold(v, rows):
    return jnp.sum(v.reshape(v.shape[0] // rows, rows, v.shape[1]), axis=0)


def join_columns(place_ref, own_ref, other_ref, out_ref, order=range(NZ)):
    for side, ref in enumerate((own_ref, other_ref)):
        half = lax.rem(place_ref[1] + side, NC) * NZ
        for i, z in enumerate(order):
            out_ref[:, pl.ds(pl.multiple_of((half + z) * LANES, LANES), LANES)] = ref[i]


def to_all(acc, out_ref, n):
    total = jnp.sum(acc, axis=0, keepdims=True)
    count = total.shape[1] // LANES
    lines = jnp.concatenate([total[:, i * LANES : (i + 1) * LANES] for i in range(count)], axis=0)
    for p in range(n):
        out_ref[p, :count] = lines


def pack_kernel(t_ref, s_ref, out_ref):
    lines = t_ref.shape[0]
    for d in range(out_ref.shape[0]):
        lanes = slice(d * LANES, (d + 1) * LANES)
        out_ref[d, :lines] = t_ref[:, lanes]
        out_ref[d, lines:] = s_ref[:, lanes]


def energy_kernel(place_ref, norm_ref, t_ref, own_ref, other_ref, e_ref, out_ref, proto_ref, acc_ref, held_ref, sem_ref):
    join_columns(place_ref, own_ref, other_ref, proto_ref)
    width = e_ref.shape[1]
    tile = 256

    def copy(j):
        at = pl.ds(pl.multiple_of(j * tile, tile), tile)
        return pltpu.make_async_copy(held_ref.at[:, at], e_ref.at[:, at], sem_ref.at[j])

    def columns(j, _):
        at = pl.ds(pl.multiple_of(j * tile, tile), tile)
        dots = jnp.dot(t_ref[...], proto_ref[:, at], preferred_element_type=jnp.float32)
        energy = jnp.exp(dots * (1.0 / TEMP_T))
        held_ref[:, at] = energy
        acc_ref[:, at] = fold(energy, 8)
        copy(j).start()
        return 0

    lax.fori_loop(0, width // tile, columns, 0)
    to_all(acc_ref[...], out_ref, out_ref.shape[0])
    for p in range(out_ref.shape[0]):
        out_ref[p, width // LANES : width // LANES + 1] = norm_ref[...]
    for j in range(width // tile):
        copy(j).wait()


def fetch(e_ref, held_ref, sem_ref):
    blocks = e_ref.shape[0] // LANES

    def copy(b):
        at = pl.ds(pl.multiple_of(b * LANES, LANES), LANES)
        return pltpu.make_async_copy(e_ref.at[at], held_ref.at[at], sem_ref.at[b])

    for b in range(blocks):
        copy(b).start()
    return blocks, lambda b: copy(b).wait()


def by_row_kernel(got_ref, e_ref, *refs):
    more = refs[:-5]
    recip_ref, out_ref, lines_ref, held_ref, sem_ref = refs[-5:]
    blocks, wait = fetch(e_ref, held_ref, sem_ref)
    width = e_ref.shape[1]
    count = width // LANES
    recip = 1.0 / jnp.sum(got_ref[:, :count], axis=0)
    for i in range(count):
        recip_ref[:, i * LANES : (i + 1) * LANES] = recip[i : i + 1, :]

    def block(b, _):
        wait(b)
        at = pl.ds(pl.multiple_of(b * LANES, LANES), LANES)
        acc = jnp.zeros((LANES, LANES), jnp.float32)
        for j in range(width // LANES):
            lanes = slice(j * LANES, (j + 1) * LANES)
            acc += held_ref[at, lanes] * recip_ref[:, lanes]
        lines_ref[pl.ds(b, 1), :] = jnp.sum(jnp.transpose(acc), axis=0, keepdims=True)
        return 0

    lax.fori_loop(0, blocks, block, 0)
    for p in range(out_ref.shape[0]):
        out_ref[p, :8] = lines_ref[...]
        at = 8
        for ref in more:
            out_ref[p, at : at + ref.shape[0]] = ref[...]
            at += ref.shape[0]


def by_column_kernel(got_ref, e_ref, out_ref, lines_ref, acc_ref, held_ref, sem_ref):
    blocks, wait = fetch(e_ref, held_ref, sem_ref)
    width = e_ref.shape[1]
    lines_ref[...] = 1.0 / jnp.sum(got_ref[...], axis=0)
    acc_ref[...] = jnp.zeros_like(acc_ref)

    def block(b, _):
        wait(b)
        at = pl.ds(pl.multiple_of(b * LANES, LANES), LANES)
        scale = down(lines_ref[pl.ds(b, 1), :])
        for j in range(width // LANES):
            lanes = slice(j * LANES, (j + 1) * LANES)
            acc_ref[:, lanes] += fold(held_ref[at, lanes] * scale, 8)
        return 0

    lax.fori_loop(0, blocks, block, 0)
    to_all(acc_ref[...], out_ref, out_ref.shape[0])


def student_sums(s_ref, proto_ref, sums_ref):
    width = proto_ref.shape[1]

    def block(b, _):
        at = pl.ds(pl.multiple_of(b * 2 * LANES, 2 * LANES), 2 * LANES)
        acc = jnp.zeros((2 * LANES, LANES), jnp.float32)
        for j in range(width // 256):
            dots = jnp.dot(
                s_ref[at, :], proto_ref[:, j * 256 : (j + 1) * 256], preferred_element_type=jnp.float32
            )
            powers = jnp.exp2(dots * (LOG2E / TEMP_S))
            acc += powers[:, :LANES] + powers[:, LANES:]
        for i in range(2):
            part = acc[i * LANES : (i + 1) * LANES]
            sums_ref[pl.ds(b * 2 + i, 1), :] = jnp.sum(jnp.transpose(part), axis=0, keepdims=True)
        return 0

    lax.fori_loop(0, s_ref.shape[0] // (2 * LANES), block, 0)


def student_kernel(place_ref, s_ref, own_ref, other_ref, proto_ref, sums_ref):
    join_columns(place_ref, own_ref, other_ref, proto_ref, BY_BITS)
    student_sums(s_ref, proto_ref, sums_ref)


def slope_kernel(
    factor, place_ref, got_ref, recip_ref, s_ref, st_ref, ps_ref, psp_ref, e_ref,
    ug_ref, keep_ref, give_ref, slope_ref, total_ref, lines_ref, down_ref,
):
    rows = st_ref.shape[2]
    width = ps_ref.shape[1]
    images = rows // CROPS
    tile = 1024
    g = pl.program_id(0)
    groups = pl.num_programs(0) - 1

    @pl.when(g == 0)
    def _():
        lines_ref[...] = factor / jnp.sum(got_ref[...], axis=0)
        total_ref[...] = jnp.zeros_like(total_ref)
        slope_ref[1] = jnp.zeros_like(slope_ref[1])

    def products(slot):
        total_ref[...] += jnp.dot(st_ref[0], slope_ref[slot], preferred_element_type=jnp.float32)
        unit = lax.dot_general(
            slope_ref[slot], ps_ref[...], (((1,), (1,)), ((), ())), preferred_element_type=jnp.float32
        )
        part = images // NY
        for crop in range(CROPS):
            for y in range(NY):
                ug_ref[0, y, crop * part : (crop + 1) * part, :] = unit[crop * images + y * part :][:part]

    def slopes_into(slot):
        for i in range(2):
            down_ref[i] = down(lines_ref[pl.ds(g * 2 + i, 1), :])
        for crop in range(CROPS):
            line = down(lines_ref[pl.ds(groups * 2 + g * CROPS + crop, 1), :])
            down_ref[2 + crop] = line if crop < 2 else 2.0 * line
        for j in range(width // tile):
            at = slice(j * tile, (j + 1) * tile)
            wide = lambda i: jnp.concatenate([down_ref[i]] * (tile // LANES), axis=1)
            recip = recip_ref[:, at]
            t0 = e_ref[:images, at] * recip * wide(0)
            t1 = e_ref[images:, at] * recip * wide(1)
            both = t0 + t1
            scores = jnp.dot(s_ref[0], ps_ref[:, at], preferred_element_type=jnp.float32)
            for crop in range(CROPS):
                lines = slice(crop * images, (crop + 1) * images)
                part = wide(2 + crop) * jnp.exp2(scores[lines] * (LOG2E / TEMP_S))
                minus = t1 if crop == 0 else t0 if crop == 1 else both
                slope_ref[slot, lines, at] = (part - minus).astype(jnp.bfloat16)

    for slot in range(2):

        @pl.when((g < groups) & (g % 2 == slot))
        def _():
            slopes_into(slot)
            products(1 - slot)

    @pl.when(g == groups)
    def _():
        products((NX - 1) % 2)

    @pl.when(g == groups)
    def _():
        blocks = width // LANES
        part = total_ref.shape[0] // (NC * NZ)
        size = blocks * part
        for b in range(blocks):
            lanes = slice(b * LANES, (b + 1) * LANES)
            dot = jnp.sum(psp_ref[:, lanes].astype(jnp.float32) * total_ref[:, lanes], axis=0, keepdims=True)
            keep_ref[NZ * size + b : NZ * size + b + 1, :] = dot
            give_ref[NZ * size + b : NZ * size + b + 1, :] = dot
        for side, ref in enumerate((keep_ref, give_ref)):
            half = lax.rem(place_ref[1] + side, NC) * NZ
            for k in range(NZ):
                z = lax.rem(place_ref[0] + k, NZ)
                lines = total_ref[pl.ds(pl.multiple_of((half + z) * part, part), part), :]
                for b in range(blocks):
                    at = k * size + b * part
                    ref[at : at + part, :] = lines[:, b * LANES : (b + 1) * LANES]


def local(teacher_feats, student_embeddings, teacher_weight, student_weight):
    images, _, bottleneck = teacher_feats.shape
    rows_here, wide = student_weight.shape
    sub = wide // (NX * NZ * NC)
    width = wide // NX
    total_k = wide * NY
    s_rows = images * CROPS
    t_rows = images * 2
    f32, bf16 = jnp.float32, jnp.bfloat16
    shape = jax.ShapeDtypeStruct
    place = jnp.stack([lax.axis_index("z"), lax.axis_index("core")]).astype(jnp.int32)
    exact = NX * t_rows * width

    t_float = teacher_feats.transpose(1, 0, 2).reshape(t_rows, bottleneck).astype(f32)
    t_unit = (t_float / jnp.sqrt(jnp.sum(t_float * t_float, axis=1, keepdims=True) + EPS)).astype(bf16)

    (shards,) = call(
        pack_kernel, [shape((NX * NZ * NC, 2 * rows_here, sub), f32)], [VMEM, VMEM], limit=58
    )(teacher_weight, student_weight)
    moved, t_unit = lax.optimization_barrier((swap(shards, DP), t_unit))
    t_all = along(t_unit, "x", NX).reshape(NX * t_rows, bottleneck)
    moved = moved.reshape(NX * NZ * NC, 2, rows_here, sub)
    cols_t = moved[:, 0].reshape(bottleneck, sub)
    cols_s = moved[:, 1].reshape(bottleneck, sub)
    col_t = jnp.sqrt(jnp.sum(cols_t * cols_t, axis=0) + EPS)
    col_s = jnp.sqrt(jnp.sum(cols_s * cols_s, axis=0) + EPS)
    mine_t = (cols_t / col_t).astype(bf16)
    mine_s = (cols_s / col_s).astype(bf16)

    s_raw = student_embeddings.transpose(1, 0, 2).reshape(s_rows, bottleneck).astype(f32)
    s_norm = jnp.sqrt(jnp.sum(s_raw * s_raw, axis=1, keepdims=True) + EPS)
    s_float = s_raw / s_norm
    s_unit, mine_t, mine_s = lax.optimization_barrier((s_float.astype(bf16), mine_t, mine_s))
    pair = exchanged(mine_s[None], "z", NZ, 4)
    s_pair = exchanged(s_unit[None], "x", NX, 1)
    own_t = spread(mine_t, "z", NZ)
    energy, to_devices = call(
        energy_kernel,
        [pltpu.HBM((NX * t_rows, width), f32), shape((NZ * NC, width // LANES + 8, LANES), f32)],
        [SMEM, VMEM, VMEM, VMEM, VMEM],
        [
            pltpu.VMEM((bottleneck, width), bf16),
            pltpu.VMEM((8, width), f32),
            pltpu.VMEM((NX * t_rows, width), f32),
            pltpu.SemaphoreType.DMA((width // 256,)),
        ],
        [HBM, VMEM],
        limit=24,
        flops=2 * exact * bottleneck,
        exps=exact,
    )(place, col_s.reshape(1, sub), t_all, own_t, other_core(own_t))

    energy = pltpu.with_memory_space_constraint(energy, pltpu.HBM)
    blocks = NX * t_rows // LANES
    held = [pltpu.VMEM((NX * t_rows, width), f32), pltpu.SemaphoreType.DMA((blocks,))]
    quarter = images // NY
    first = lax.axis_index("proto") * quarter
    part_float = lax.dynamic_slice_in_dim(s_float.reshape(CROPS, images, bottleneck), first, quarter, 1)
    part_norm = lax.dynamic_slice_in_dim(s_norm.reshape(CROPS, images, 1), first, quarter, 1)
    part_float, part_norm, to_devices = lax.optimization_barrier((part_float, part_norm, to_devices))

    def by_row(got, *more):
        lines = 8 + sum(m.shape[0] for m in more)
        return call(
            by_row_kernel,
            [shape((1, width), f32), shape((NX * NY, lines, LANES), f32)],
            [VMEM, HBM] + [VMEM] * len(more),
            [pltpu.VMEM((8, LANES), f32)] + held,
            limit=12,
            flops=2 * exact,
            moved=4 * exact,
        )(got, energy, *more)

    def by_column(got):
        (to_devices,) = call(
            by_column_kernel,
            [shape((NZ * NC, width // LANES, LANES), f32)],
            [VMEM, HBM],
            [pltpu.VMEM((8, LANES), f32), pltpu.VMEM((8, width), f32)] + held,
            limit=12,
            flops=2 * exact,
            moved=4 * exact,
        )(got, energy)
        return to_devices

    half_rows = NX * s_rows // 2
    student = dict(limit=20, flops=exact * 3 * bottleneck, exps=exact * 3 // 2)

    to_devices, own_s = lax.optimization_barrier((to_devices, merged(pair, "z", 4)))
    got = swap(to_devices, ZC)
    pair = exchanged(own_s, "z", NZ, 1)
    col_s = got[:, width // LANES].reshape(NZ, NC, LANES).transpose(1, 0, 2).reshape(NZ * NC, 1, LANES)
    _, to_devices = by_row(got)
    to_devices, own_s, s_all = lax.optimization_barrier((to_devices, merged(pair, "z", 1), merged(s_pair, "x", 1)))
    got = swap(to_devices, XY)
    pair = exchanged(own_s, "z", NZ, 2)
    to_devices = by_column(got)

    to_devices, own_s, s_all = lax.optimization_barrier((to_devices, merged(pair, "z", 2), s_all))
    got = swap(to_devices, ZC)
    other_s = other_core(own_s)
    s_pair = exchanged(s_all, "x", NX, 2)
    _, to_devices = by_row(got)
    to_devices, other_s, s_pair = lax.optimization_barrier((to_devices, other_s, s_pair))
    got = swap(to_devices, XY)
    s_all = merged(s_pair, "x", 2)
    s_halves = s_all.reshape(2, half_rows, bottleneck)
    proto_s, first_sums = call(
        student_kernel,
        [shape((bottleneck, width), bf16), shape((half_rows // LANES, LANES), f32)],
        [SMEM, VMEM, VMEM, VMEM],
        **student,
    )(place, s_halves[0], own_s, other_s)
    to_devices = by_column(got)

    to_devices, proto_s, s_all, first_sums = lax.optimization_barrier((to_devices, proto_s, s_all, first_sums))
    got = swap(to_devices, ZC)
    (last_sums,) = call(
        student_sums, [shape((half_rows // LANES, LANES), f32)], [VMEM, VMEM], **student
    )(s_all.reshape(2, half_rows, bottleneck)[1], proto_s)
    recip, to_devices = by_row(got, first_sums, last_sums)
    to_devices, proto_s, s_all = lax.optimization_barrier((to_devices, proto_s, s_all))
    got = swap(to_devices, XY)

    order = jnp.arange(bottleneck).reshape(NX, NZ, NC, rows_here).transpose(2, 1, 0, 3).reshape(-1)
    ordered = (order[:, None] == jnp.arange(bottleneck)[None, :]).astype(bf16)
    proto_o = jnp.dot(ordered, proto_s, preferred_element_type=f32).astype(bf16)
    s_o = jnp.einsum("pb,grb->gpr", ordered, s_all, preferred_element_type=f32).astype(bf16)
    size = bottleneck * width // (NC * NZ * LANES)
    unit_part, keep, give = call(
        functools.partial(slope_kernel, total_k / 16.0),
        [pltpu.VMEM((NX, NY, s_rows // NY, bottleneck), f32)] + [pltpu.HBM((NZ * size + width // LANES, LANES), f32)] * NC,
        [
            SMEM,
            whole(NX * NY, NX * (2 + CROPS), LANES),
            whole(1, width),
            pl.BlockSpec((1, s_rows, bottleneck), lambda g: (jnp.minimum(g, NX - 1), 0, 0)),
            pl.BlockSpec((1, bottleneck, s_rows), lambda g: (jnp.maximum(g - 1, 0), 0, 0)),
            whole(bottleneck, width),
            whole(bottleneck, width),
            pl.BlockSpec((t_rows, width), lambda g: (jnp.minimum(g, NX - 1), 0)),
        ],
        [
            pltpu.VMEM((2, s_rows, width), bf16),
            pltpu.VMEM((bottleneck, width), f32),
            pltpu.VMEM((NX * (2 + CROPS), LANES), f32),
            pltpu.VMEM((2 + CROPS, LANES, LANES), f32),
        ],
        [
            pl.BlockSpec((1, NY, s_rows // NY, bottleneck), lambda g: (jnp.maximum(g - 1, 0), 0, 0, 0)),
            whole(NZ * size + width // LANES, LANES),
            whole(NZ * size + width // LANES, LANES),
        ],
        (NX + 1,),
        limit=40,
        flops=6 * exact * 3 * bottleneck,
        moved=4 * exact,
        exps=exact * 3,
    )(
        place,
        pltpu.with_memory_space_constraint(got, pltpu.HBM),
        recip,
        *(pltpu.with_memory_space_constraint(v, pltpu.HBM) for v in (s_all, s_o, proto_s, proto_o)),
        energy,
    )

    half = (keep + other_core(give)) * (1.0 / 512.0)
    dots = half[NZ * size :]
    high = lax.reduce_precision(dots, 5, 10)
    ends = [high.astype(jnp.float16), ((dots - high) * 1024.0).astype(jnp.float16)]
    proto_grad = half[:size]
    for k in range(1, NZ):
        sent = jnp.concatenate([half[k * size : (k + 1) * size].astype(jnp.float16)] + ends)
        came = shifted(sent, "z", NZ, k).astype(f32)
        proto_grad = proto_grad + came[:size]
        dots = dots + (came[size : size + NZ * NC] + came[size + NZ * NC :] * (1.0 / 1024.0))
    lines = bottleneck // (NC * NZ)
    proto_grad = proto_grad.reshape(NC * NZ, lines, LANES) * 512.0
    column_dot = dots.reshape(NC * NZ, 1, LANES) * 512.0
    at = (lax.axis_index("core") * NZ + lax.axis_index("z")) * lines
    proto_float = lax.dynamic_slice_in_dim(proto_o, at, lines, 0).astype(f32)
    proto_float = proto_float.reshape(lines, NC * NZ, LANES).transpose(1, 0, 2)
    grad_lines = (proto_grad - proto_float * column_dot) / col_s

    sent = (unit_part.reshape(NX * NY, CROPS * quarter, bottleneck) * 4.0).astype(jnp.float16)
    unit_grad = jnp.sum(swap(sent, XY).astype(f32), axis=0) * 0.25
    unit_grad = unit_grad.reshape(CROPS, quarter, bottleneck)
    fgrad = (unit_grad - part_float * jnp.sum(part_float * unit_grad, axis=2, keepdims=True)) / part_norm

    grad_lines, fgrad = lax.optimization_barrier((grad_lines, fgrad))
    feature_grad = along(fgrad.transpose(1, 0, 2), "proto", NY).reshape(images, CROPS, bottleneck)
    grad_lines = grad_lines.reshape(NC * NZ, NX, rows_here, LANES).transpose(1, 0, 2, 3)
    grad_rows = swap(grad_lines, "x").reshape(NX, NC, NZ, rows_here, LANES)
    weight_grad = grad_rows.transpose(3, 0, 2, 1, 4).reshape(rows_here, wide)
    teacher_new = 0.994 * teacher_weight + 0.006 * (student_weight - 0.5 * weight_grad)
    return weight_grad, teacher_new, feature_grad


def solution(mesh):
    fine = Mesh(mesh.devices.reshape(NX, NZ, NC, NY), ("x", "z", "core", "proto"))
    in_specs = (P(DP, None, None), P(DP, None, None), P(DP, "proto"), P(DP, "proto"))
    out_specs = (P(DP, "proto"), P(DP, "proto"), P(DP, None, None))
    return jax.shard_map(local, mesh=fine, in_specs=in_specs, out_specs=out_specs, check_vma=False)
```

```python
import jax
import jax.numpy as jnp
from jax import lax
from jax.experimental import pallas as pl
from jax.experimental.pallas import tpu as pltpu
from jax.sharding import Mesh, PartitionSpec as P

BALANCING_ROUNDS = 3
EPS = 1e-06
TEMP_T = 0.07
TEMP_S = 0.1
CROPS = 6
NX, NZ, NC, NY = 4, 8, 2, 4
DP = ("x", "z", "core")
XY = ("x", "proto")
ZC = ("z", "core")
LANES = 128
BY_BITS = [b4 * 4 + b2 * 2 + b1 for b2 in range(2) for b1 in range(2) for b4 in range(2)]
LOG2E = 1.4426950408889634
MIB = 1024 * 1024
VMEM = pl.BlockSpec(memory_space=pltpu.VMEM)
SMEM = pl.BlockSpec(memory_space=pltpu.SMEM)
HBM = pl.BlockSpec(memory_space=pltpu.HBM)


def swap(v, axes):
    return lax.all_to_all(v, axes, 0, 0)


def spread(v, axes, n):
    return swap(jnp.broadcast_to(v, (n,) + v.shape), axes)


def other_core(v):
    return lax.ppermute(v, "core", [(0, 1), (1, 0)])


def shifted(v, axis, n, k):
    return lax.ppermute(v, axis, [(i, (i + k) % n) for i in range(n)])


def along(v, axis, n):
    me = lax.axis_index(axis)
    out = jnp.zeros((n,) + v.shape, v.dtype)
    for k in range(n):
        part = v if k == 0 else shifted(v, axis, n, k)
        out = lax.dynamic_update_index_in_dim(out, part, (me - k) % n, 0)
    return out


def exchanged(v, axis, n, step):
    return v, lax.ppermute(v, axis, [(i, i ^ step) for i in range(n)])


def merged(pair, axis, step):
    own, got = pair
    high = (lax.axis_index(axis) // step) % 2 == 1
    return jnp.concatenate([jnp.where(high, got, own), jnp.where(high, own, got)])


def whole(*shape):
    return pl.BlockSpec(shape, lambda *at: (0,) * len(shape))


def call(kernel, out_shape, in_specs, scratch=(), out_specs=None, grid=(), limit=8, flops=0, moved=0, exps=0):
    return pl.pallas_call(
        kernel,
        grid=grid,
        out_shape=out_shape,
        in_specs=in_specs,
        out_specs=out_specs or [VMEM] * len(out_shape),
        scratch_shapes=list(scratch),
        compiler_params=pltpu.CompilerParams(vmem_limit_bytes=limit * MIB),
        cost_estimate=pl.CostEstimate(flops=flops, bytes_accessed=moved, transcendentals=exps),
    )


def down(row):
    return jnp.transpose(jnp.broadcast_to(row, (LANES, LANES)))


def fold(v, rows):
    return jnp.sum(v.reshape(v.shape[0] // rows, rows, v.shape[1]), axis=0)


def join_columns(place_ref, own_ref, other_ref, out_ref, order=range(NZ)):
    for side, ref in enumerate((own_ref, other_ref)):
        half = lax.rem(place_ref[1] + side, NC) * NZ
        for i, z in enumerate(order):
            out_ref[:, pl.ds(pl.multiple_of((half + z) * LANES, LANES), LANES)] = ref[i]


def to_all(acc, out_ref, n):
    total = jnp.sum(acc, axis=0, keepdims=True)
    count = total.shape[1] // LANES
    lines = jnp.concatenate([total[:, i * LANES : (i + 1) * LANES] for i in range(count)], axis=0)
    for p in range(n):
        out_ref[p, :count] = lines


def pack_kernel(t_ref, s_ref, out_ref):
    lines = t_ref.shape[0]
    for d in range(out_ref.shape[0]):
        lanes = slice(d * LANES, (d + 1) * LANES)
        out_ref[d, :lines] = t_ref[:, lanes]
        out_ref[d, lines:] = s_ref[:, lanes]


def energy_kernel(place_ref, norm_ref, t_ref, own_ref, other_ref, e_ref, out_ref, proto_ref, acc_ref, held_ref, sem_ref):
    join_columns(place_ref, own_ref, other_ref, proto_ref)
    width = e_ref.shape[1]
    tile = 512

    def copy(j):
        at = pl.ds(pl.multiple_of(j * tile, tile), tile)
        return pltpu.make_async_copy(held_ref.at[:, at], e_ref.at[:, at], sem_ref.at[j])

    def columns(j, _):
        at = pl.ds(pl.multiple_of(j * tile, tile), tile)
        dots = jnp.dot(t_ref[...], proto_ref[:, at], preferred_element_type=jnp.float32)
        energy = jnp.exp2(dots * (LOG2E / TEMP_T))
        held_ref[:, at] = energy
        acc_ref[:, at] = fold(energy, 8)
        copy(j).start()
        return 0

    lax.fori_loop(0, width // tile, columns, 0, unroll=True)
    to_all(acc_ref[...], out_ref, out_ref.shape[0])
    for p in range(out_ref.shape[0]):
        out_ref[p, width // LANES : width // LANES + 1] = norm_ref[...]
    for j in range(width // tile):
        copy(j).wait()


def fetch(e_ref, held_ref, sem_ref):
    blocks = e_ref.shape[0] // LANES

    def copy(b):
        at = pl.ds(pl.multiple_of(b * LANES, LANES), LANES)
        return pltpu.make_async_copy(e_ref.at[at], held_ref.at[at], sem_ref.at[b])

    for b in range(blocks):
        copy(b).start()
    return blocks, lambda b: copy(b).wait()


def by_row_kernel(got_ref, e_ref, *refs):
    more = refs[:-5]
    recip_ref, out_ref, lines_ref, held_ref, sem_ref = refs[-5:]
    blocks, wait = fetch(e_ref, held_ref, sem_ref)
    width = e_ref.shape[1]
    count = width // LANES
    recip = 1.0 / jnp.sum(got_ref[:, :count], axis=0)
    for i in range(count):
        recip_ref[:, i * LANES : (i + 1) * LANES] = recip[i : i + 1, :]

    def block(b, _):
        wait(b)
        at = pl.ds(pl.multiple_of(b * LANES, LANES), LANES)
        acc = jnp.zeros((LANES, LANES), jnp.float32)
        for j in range(width // LANES):
            lanes = slice(j * LANES, (j + 1) * LANES)
            acc += held_ref[at, lanes] * recip_ref[:, lanes]
        lines_ref[pl.ds(b, 1), :] = jnp.sum(jnp.transpose(acc), axis=0, keepdims=True)
        return 0

    lax.fori_loop(0, blocks, block, 0)
    for p in range(out_ref.shape[0]):
        out_ref[p, :8] = lines_ref[...]
        at = 8
        for ref in more:
            out_ref[p, at : at + ref.shape[0]] = ref[...]
            at += ref.shape[0]


def by_column_kernel(got_ref, e_ref, out_ref, lines_ref, acc_ref, held_ref, sem_ref):
    blocks, wait = fetch(e_ref, held_ref, sem_ref)
    width = e_ref.shape[1]
    lines_ref[...] = 1.0 / jnp.sum(got_ref[...], axis=0)
    acc_ref[...] = jnp.zeros_like(acc_ref)

    def block(b, _):
        wait(b)
        at = pl.ds(pl.multiple_of(b * LANES, LANES), LANES)
        scale = down(lines_ref[pl.ds(b, 1), :])
        for j in range(width // LANES):
            lanes = slice(j * LANES, (j + 1) * LANES)
            acc_ref[:, lanes] += fold(held_ref[at, lanes] * scale, 8)
        return 0

    lax.fori_loop(0, blocks, block, 0)
    to_all(acc_ref[...], out_ref, out_ref.shape[0])


def student_sums(s_ref, proto_ref, sums_ref):
    width = proto_ref.shape[1]

    def block(b, _):
        at = pl.ds(pl.multiple_of(b * 2 * LANES, 2 * LANES), 2 * LANES)
        acc = jnp.zeros((2 * LANES, LANES), jnp.float32)
        for j in range(width // 256):
            dots = jnp.dot(
                s_ref[at, :], proto_ref[:, j * 256 : (j + 1) * 256], preferred_element_type=jnp.float32
            )
            powers = jnp.exp2(dots * (LOG2E / TEMP_S))
            acc += powers[:, :LANES] + powers[:, LANES:]
        for i in range(2):
            part = acc[i * LANES : (i + 1) * LANES]
            sums_ref[pl.ds(b * 2 + i, 1), :] = jnp.sum(jnp.transpose(part), axis=0, keepdims=True)
        return 0

    lax.fori_loop(0, s_ref.shape[0] // (2 * LANES), block, 0)


def student_kernel(place_ref, s_ref, own_ref, other_ref, proto_ref, sums_ref):
    join_columns(place_ref, own_ref, other_ref, proto_ref, BY_BITS)
    student_sums(s_ref, proto_ref, sums_ref)


def slope_kernel(
    place_ref, lines_ref, recip_ref, s_ref, st_ref, ps_ref, psp_ref, e_ref,
    ug_ref, keep_ref, give_ref, slope_ref, total_ref, down_ref,
):
    rows = st_ref.shape[2]
    width = ps_ref.shape[1]
    images = rows // CROPS
    tile = 1024
    g = pl.program_id(0)
    groups = pl.num_programs(0) - 1

    @pl.when(g == 0)
    def _():
        total_ref[...] = jnp.zeros_like(total_ref)
        slope_ref[1] = jnp.zeros_like(slope_ref[1])

    def products(slot):
        total_ref[...] += jnp.dot(st_ref[0], slope_ref[slot], preferred_element_type=jnp.float32)
        unit = lax.dot_general(
            slope_ref[slot], ps_ref[...], (((1,), (1,)), ((), ())), preferred_element_type=jnp.float32
        )
        part = images // NY
        for crop in range(CROPS):
            for y in range(NY):
                ug_ref[0, y, crop * part : (crop + 1) * part, :] = unit[crop * images + y * part :][:part]

    def slopes_into(slot):
        for i in range(2):
            down_ref[i] = down(lines_ref[pl.ds(g * 2 + i, 1), :])
        for crop in range(CROPS):
            line = down(lines_ref[pl.ds(groups * 2 + g * CROPS + crop, 1), :])
            down_ref[2 + crop] = line if crop < 2 else 2.0 * line
        for j in range(width // tile):
            at = slice(j * tile, (j + 1) * tile)
            wide = lambda i: jnp.concatenate([down_ref[i]] * (tile // LANES), axis=1)
            recip = recip_ref[:, at]
            t0 = e_ref[:images, at] * recip * wide(0)
            t1 = e_ref[images:, at] * recip * wide(1)
            both = t0 + t1
            scores = jnp.dot(s_ref[0], ps_ref[:, at], preferred_element_type=jnp.float32)
            for crop in range(CROPS):
                lines = slice(crop * images, (crop + 1) * images)
                part = wide(2 + crop) * jnp.exp2(scores[lines] * (LOG2E / TEMP_S))
                minus = t1 if crop == 0 else t0 if crop == 1 else both
                slope_ref[slot, lines, at] = (part - minus).astype(jnp.bfloat16)

    for slot in range(2):

        @pl.when((g < groups) & (g % 2 == slot))
        def _():
            slopes_into(slot)
            products(1 - slot)

    @pl.when(g == groups)
    def _():
        products((NX - 1) % 2)

    @pl.when(g == groups)
    def _():
        blocks = width // LANES
        part = total_ref.shape[0] // (NC * NZ)
        size = blocks * part
        for b in range(blocks):
            lanes = slice(b * LANES, (b + 1) * LANES)
            dot = jnp.sum(psp_ref[:, lanes].astype(jnp.float32) * total_ref[:, lanes], axis=0, keepdims=True)
            keep_ref[NZ * size + b : NZ * size + b + 1, :] = dot
            give_ref[NZ * size + b : NZ * size + b + 1, :] = dot
        for side, ref in enumerate((keep_ref, give_ref)):
            half = lax.rem(place_ref[1] + side, NC) * NZ
            for k in range(NZ):
                z = lax.rem(place_ref[0] + k, NZ)
                lines = total_ref[pl.ds(pl.multiple_of((half + z) * part, part), part), :]
                for b in range(blocks):
                    at = k * size + b * part
                    ref[at : at + part, :] = lines[:, b * LANES : (b + 1) * LANES]


def local(teacher_feats, student_embeddings, teacher_weight, student_weight):
    images, _, bottleneck = teacher_feats.shape
    rows_here, wide = student_weight.shape
    sub = wide // (NX * NZ * NC)
    width = wide // NX
    total_k = wide * NY
    s_rows = images * CROPS
    t_rows = images * 2
    f32, bf16 = jnp.float32, jnp.bfloat16
    shape = jax.ShapeDtypeStruct
    place = jnp.stack([lax.axis_index("z"), lax.axis_index("core")]).astype(jnp.int32)
    exact = NX * t_rows * width

    t_float = teacher_feats.transpose(1, 0, 2).reshape(t_rows, bottleneck).astype(f32)
    t_unit = (t_float / jnp.sqrt(jnp.sum(t_float * t_float, axis=1, keepdims=True) + EPS)).astype(bf16)

    (shards,) = call(
        pack_kernel, [shape((NX * NZ * NC, 2 * rows_here, sub), f32)], [VMEM, VMEM], limit=58
    )(teacher_weight, student_weight)
    moved, t_unit = lax.optimization_barrier((swap(shards, DP), t_unit))
    t_all = along(t_unit, "x", NX).reshape(NX * t_rows, bottleneck)
    moved = moved.reshape(NX * NZ * NC, 2, rows_here, sub)
    cols_t = moved[:, 0].reshape(bottleneck, sub)
    cols_s = moved[:, 1].reshape(bottleneck, sub)
    col_t = jnp.sqrt(jnp.sum(cols_t * cols_t, axis=0) + EPS)
    col_s = jnp.sqrt(jnp.sum(cols_s * cols_s, axis=0) + EPS)
    mine_t = (cols_t / col_t).astype(bf16)
    mine_s = (cols_s / col_s).astype(bf16)

    s_raw = student_embeddings.transpose(1, 0, 2).reshape(s_rows, bottleneck).astype(f32)
    s_norm = jnp.sqrt(jnp.sum(s_raw * s_raw, axis=1, keepdims=True) + EPS)
    s_float = s_raw / s_norm
    s_unit, mine_t, mine_s = lax.optimization_barrier((s_float.astype(bf16), mine_t, mine_s))
    pair = exchanged(mine_s[None], "z", NZ, 4)
    s_pair = exchanged(s_unit[None], "x", NX, 1)
    own_t = spread(mine_t, "z", NZ)
    energy, to_devices = call(
        energy_kernel,
        [pltpu.HBM((NX * t_rows, width), f32), shape((NZ * NC, width // LANES + 8, LANES), f32)],
        [SMEM, VMEM, VMEM, VMEM, VMEM],
        [
            pltpu.VMEM((bottleneck, width), bf16),
            pltpu.VMEM((8, width), f32),
            pltpu.VMEM((NX * t_rows, width), f32),
            pltpu.SemaphoreType.DMA((width // 512,)),
        ],
        [HBM, VMEM],
        limit=24,
        flops=2 * exact * bottleneck,
        exps=exact,
    )(place, col_s.reshape(1, sub), t_all, own_t, other_core(own_t))

    energy = pltpu.with_memory_space_constraint(energy, pltpu.HBM)
    blocks = NX * t_rows // LANES
    held = [pltpu.VMEM((NX * t_rows, width), f32), pltpu.SemaphoreType.DMA((blocks,))]
    quarter = images // NY
    first = lax.axis_index("proto") * quarter
    part_float = lax.dynamic_slice_in_dim(s_float.reshape(CROPS, images, bottleneck), first, quarter, 1)
    part_norm = lax.dynamic_slice_in_dim(s_norm.reshape(CROPS, images, 1), first, quarter, 1)
    part_float, part_norm, to_devices = lax.optimization_barrier((part_float, part_norm, to_devices))

    def by_row(got, *more):
        lines = 8 + sum(m.shape[0] for m in more)
        return call(
            by_row_kernel,
            [shape((1, width), f32), shape((NX * NY, lines, LANES), f32)],
            [VMEM, HBM] + [VMEM] * len(more),
            [pltpu.VMEM((8, LANES), f32)] + held,
            limit=12,
            flops=2 * exact,
            moved=4 * exact,
        )(got, energy, *more)

    def by_column(got):
        (to_devices,) = call(
            by_column_kernel,
            [shape((NZ * NC, width // LANES, LANES), f32)],
            [VMEM, HBM],
            [pltpu.VMEM((8, LANES), f32), pltpu.VMEM((8, width), f32)] + held,
            limit=12,
            flops=2 * exact,
            moved=4 * exact,
        )(got, energy)
        return to_devices

    half_rows = NX * s_rows // 2
    student = dict(limit=20, flops=exact * 3 * bottleneck, exps=exact * 3 // 2)

    to_devices, own_s = lax.optimization_barrier((to_devices, merged(pair, "z", 4)))
    got = swap(to_devices, ZC)
    pair = exchanged(own_s, "z", NZ, 1)
    col_s = got[:, width // LANES].reshape(NZ, NC, LANES).transpose(1, 0, 2).reshape(NZ * NC, 1, LANES)
    _, to_devices = by_row(got)
    to_devices, own_s, s_all = lax.optimization_barrier((to_devices, merged(pair, "z", 1), merged(s_pair, "x", 1)))
    got = swap(to_devices, XY)
    pair = exchanged(own_s, "z", NZ, 2)
    to_devices = by_column(got)

    to_devices, own_s, s_all = lax.optimization_barrier((to_devices, merged(pair, "z", 2), s_all))
    got = swap(to_devices, ZC)
    other_s = other_core(own_s)
    s_pair = exchanged(s_all, "x", NX, 2)
    _, to_devices = by_row(got)
    to_devices, other_s, s_pair = lax.optimization_barrier((to_devices, other_s, s_pair))
    got = swap(to_devices, XY)
    s_all = merged(s_pair, "x", 2)
    s_halves = s_all.reshape(2, half_rows, bottleneck)
    proto_s, first_sums = call(
        student_kernel,
        [shape((bottleneck, width), bf16), shape((half_rows // LANES, LANES), f32)],
        [SMEM, VMEM, VMEM, VMEM],
        **student,
    )(place, s_halves[0], own_s, other_s)
    to_devices = by_column(got)

    to_devices, proto_s, s_all, first_sums = lax.optimization_barrier((to_devices, proto_s, s_all, first_sums))
    got = swap(to_devices, ZC)
    (last_sums,) = call(
        student_sums, [shape((half_rows // LANES, LANES), f32)], [VMEM, VMEM], **student
    )(s_all.reshape(2, half_rows, bottleneck)[1], proto_s)
    recip, to_devices = by_row(got, first_sums, last_sums)
    to_devices, proto_s, s_all = lax.optimization_barrier((to_devices, proto_s, s_all))
    got = swap(to_devices, XY)

    order = jnp.arange(bottleneck).reshape(NX, NZ, NC, rows_here).transpose(2, 1, 0, 3).reshape(-1)
    ordered = (order[:, None] == jnp.arange(bottleneck)[None, :]).astype(bf16)
    proto_o = jnp.dot(ordered, proto_s, preferred_element_type=f32).astype(bf16)
    s_o = jnp.einsum("pb,grb->gpr", ordered, s_all, preferred_element_type=f32).astype(bf16)
    size = bottleneck * width // (NC * NZ * LANES)
    unit_part, keep, give = call(
        slope_kernel,
        [pltpu.VMEM((NX, NY, s_rows // NY, bottleneck), f32)] + [pltpu.HBM((NZ * size + width // LANES, LANES), f32)] * NC,
        [
            SMEM,
            whole(NX * (2 + CROPS), LANES),
            whole(1, width),
            pl.BlockSpec((1, s_rows, bottleneck), lambda g: (jnp.minimum(g, NX - 1), 0, 0)),
            pl.BlockSpec((1, bottleneck, s_rows), lambda g: (jnp.maximum(g - 1, 0), 0, 0)),
            whole(bottleneck, width),
            whole(bottleneck, width),
            pl.BlockSpec((t_rows, width), lambda g: (jnp.minimum(g, NX - 1), 0)),
        ],
        [
            pltpu.VMEM((2, s_rows, width), bf16),
            pltpu.VMEM((bottleneck, width), f32),
            pltpu.VMEM((2 + CROPS, LANES, LANES), f32),
        ],
        [
            pl.BlockSpec((1, NY, s_rows // NY, bottleneck), lambda g: (jnp.maximum(g - 1, 0), 0, 0, 0)),
            whole(NZ * size + width // LANES, LANES),
            whole(NZ * size + width // LANES, LANES),
        ],
        (NX + 1,),
        limit=40,
        flops=6 * exact * 3 * bottleneck,
        moved=4 * exact,
        exps=exact * 3,
    )(
        place,
        total_k / 16.0 / jnp.sum(got, axis=0),
        recip,
        *(pltpu.with_memory_space_constraint(v, pltpu.HBM) for v in (s_all, s_o, proto_s, proto_o)),
        energy,
    )

    half = (keep + other_core(give)) * (1.0 / 512.0)
    dots = half[NZ * size :]
    high = lax.reduce_precision(dots, 5, 10)
    ends = [high.astype(jnp.float16), ((dots - high) * 1024.0).astype(jnp.float16)]
    proto_grad = half[:size]
    for k in range(1, NZ):
        sent = jnp.concatenate([half[k * size : (k + 1) * size].astype(jnp.float16)] + ends)
        came = shifted(sent, "z", NZ, k).astype(f32)
        proto_grad = proto_grad + came[:size]
        dots = dots + (came[size : size + NZ * NC] + came[size + NZ * NC :] * (1.0 / 1024.0))
    lines = bottleneck // (NC * NZ)
    proto_grad = proto_grad.reshape(NC * NZ, lines, LANES) * 512.0
    column_dot = dots.reshape(NC * NZ, 1, LANES) * 512.0
    at = (lax.axis_index("core") * NZ + lax.axis_index("z")) * lines
    proto_float = lax.dynamic_slice_in_dim(proto_o, at, lines, 0).astype(f32)
    proto_float = proto_float.reshape(lines, NC * NZ, LANES).transpose(1, 0, 2)
    grad_lines = (proto_grad - proto_float * column_dot) / col_s

    sent = (unit_part.reshape(NX * NY, CROPS * quarter, bottleneck) * 4.0).astype(jnp.float16)
    unit_grad = jnp.sum(swap(sent, XY).astype(f32), axis=0) * 0.25
    unit_grad = unit_grad.reshape(CROPS, quarter, bottleneck)
    fgrad = (unit_grad - part_float * jnp.sum(part_float * unit_grad, axis=2, keepdims=True)) / part_norm

    grad_lines, fgrad = lax.optimization_barrier((grad_lines, fgrad))
    feature_grad = along(fgrad.transpose(1, 0, 2), "proto", NY).reshape(images, CROPS, bottleneck)
    grad_lines = grad_lines.reshape(NC * NZ, NX, rows_here, LANES).transpose(1, 0, 2, 3)
    grad_rows = swap(grad_lines, "x").reshape(NX, NC, NZ, rows_here, LANES)
    weight_grad = grad_rows.transpose(3, 0, 2, 1, 4).reshape(rows_here, wide)
    teacher_new = 0.994 * teacher_weight + 0.006 * (student_weight - 0.5 * weight_grad)
    return weight_grad, teacher_new, feature_grad


def solution(mesh):
    fine = Mesh(mesh.devices.reshape(NX, NZ, NC, NY), ("x", "z", "core", "proto"))
    in_specs = (P(DP, None, None), P(DP, None, None), P(DP, "proto"), P(DP, "proto"))
    out_specs = (P(DP, "proto"), P(DP, "proto"), P(DP, None, None))
    return jax.shard_map(local, mesh=fine, in_specs=in_specs, out_specs=out_specs, check_vma=False)
```

```python
import jax
import jax.numpy as jnp
from jax import lax
from jax.experimental import pallas as pl
from jax.experimental.pallas import tpu as pltpu
from jax.sharding import Mesh, PartitionSpec as P

BALANCING_ROUNDS = 3
EPS = 1e-06
TEMP_T = 0.07
TEMP_S = 0.1
CROPS = 6
NX, NZ, NC, NY = 4, 8, 2, 4
DP = ("x", "z", "core")
XY = ("x", "proto")
ZC = ("z", "core")
LANES = 128
BY_BITS = [b4 * 4 + b2 * 2 + b1 for b2 in range(2) for b1 in range(2) for b4 in range(2)]
LOG2E = 1.4426950408889634
MIB = 1024 * 1024
VMEM = pl.BlockSpec(memory_space=pltpu.VMEM)
SMEM = pl.BlockSpec(memory_space=pltpu.SMEM)
HBM = pl.BlockSpec(memory_space=pltpu.HBM)


def swap(v, axes):
    return lax.all_to_all(v, axes, 0, 0)


def spread(v, axes, n):
    return swap(jnp.broadcast_to(v, (n,) + v.shape), axes)


def other_core(v):
    return lax.ppermute(v, "core", [(0, 1), (1, 0)])


def shifted(v, axis, n, k):
    return lax.ppermute(v, axis, [(i, (i + k) % n) for i in range(n)])


def along(v, axis, n):
    me = lax.axis_index(axis)
    out = jnp.zeros((n,) + v.shape, v.dtype)
    for k in range(n):
        part = v if k == 0 else shifted(v, axis, n, k)
        out = lax.dynamic_update_index_in_dim(out, part, (me - k) % n, 0)
    return out


def exchanged(v, axis, n, step):
    return v, lax.ppermute(v, axis, [(i, i ^ step) for i in range(n)])


def merged(pair, axis, step):
    own, got = pair
    high = (lax.axis_index(axis) // step) % 2 == 1
    return jnp.concatenate([jnp.where(high, got, own), jnp.where(high, own, got)])


def whole(*shape):
    return pl.BlockSpec(shape, lambda *at: (0,) * len(shape))


def call(kernel, out_shape, in_specs, scratch=(), out_specs=None, grid=(), limit=8, flops=0, moved=0, exps=0):
    return pl.pallas_call(
        kernel,
        grid=grid,
        out_shape=out_shape,
        in_specs=in_specs,
        out_specs=out_specs or [VMEM] * len(out_shape),
        scratch_shapes=list(scratch),
        compiler_params=pltpu.CompilerParams(vmem_limit_bytes=limit * MIB),
        cost_estimate=pl.CostEstimate(flops=flops, bytes_accessed=moved, transcendentals=exps),
    )


def down(row):
    return jnp.transpose(jnp.broadcast_to(row, (LANES, LANES)))


def fold(v, rows):
    return jnp.sum(v.reshape(v.shape[0] // rows, rows, v.shape[1]), axis=0)


def join_columns(place_ref, own_ref, other_ref, out_ref, order=range(NZ)):
    for side, ref in enumerate((own_ref, other_ref)):
        half = lax.rem(place_ref[1] + side, NC) * NZ
        for i, z in enumerate(order):
            out_ref[:, pl.ds(pl.multiple_of((half + z) * LANES, LANES), LANES)] = ref[i]


def to_all(acc, out_ref, n):
    total = jnp.sum(acc, axis=0, keepdims=True)
    count = total.shape[1] // LANES
    lines = jnp.concatenate([total[:, i * LANES : (i + 1) * LANES] for i in range(count)], axis=0)
    for p in range(n):
        out_ref[p, :count] = lines


def pack_kernel(t_ref, s_ref, out_ref):
    lines = t_ref.shape[0]
    for d in range(out_ref.shape[0]):
        lanes = slice(d * LANES, (d + 1) * LANES)
        out_ref[d, :lines] = t_ref[:, lanes]
        out_ref[d, lines:] = s_ref[:, lanes]


def energy_kernel(place_ref, norm_ref, t_ref, own_ref, other_ref, e_ref, out_ref, proto_ref, acc_ref, held_ref, sem_ref):
    join_columns(place_ref, own_ref, other_ref, proto_ref)
    width = e_ref.shape[1]
    tile = 512

    def copy(j):
        at = pl.ds(pl.multiple_of(j * tile, tile), tile)
        return pltpu.make_async_copy(held_ref.at[:, at], e_ref.at[:, at], sem_ref.at[j])

    def columns(j, _):
        at = pl.ds(pl.multiple_of(j * tile, tile), tile)
        dots = jnp.dot(t_ref[...], proto_ref[:, at], preferred_element_type=jnp.float32)
        energy = jnp.exp2(dots * (LOG2E / TEMP_T))
        held_ref[:, at] = energy
        acc_ref[:, at] = fold(energy, 8)
        copy(j).start()
        return 0

    lax.fori_loop(0, width // tile, columns, 0, unroll=True)
    to_all(acc_ref[...], out_ref, out_ref.shape[0])
    for p in range(out_ref.shape[0]):
        out_ref[p, width // LANES : width // LANES + 1] = norm_ref[...]
    for j in range(width // tile):
        copy(j).wait()


def fetch(e_ref, held_ref, sem_ref):
    blocks = e_ref.shape[0] // LANES

    def copy(b):
        at = pl.ds(pl.multiple_of(b * LANES, LANES), LANES)
        return pltpu.make_async_copy(e_ref.at[at], held_ref.at[at], sem_ref.at[b])

    for b in range(blocks):
        copy(b).start()
    return blocks, lambda b: copy(b).wait()


def by_row_kernel(got_ref, e_ref, *refs):
    more = refs[:-5]
    recip_ref, out_ref, lines_ref, held_ref, sem_ref = refs[-5:]
    blocks, wait = fetch(e_ref, held_ref, sem_ref)
    width = e_ref.shape[1]
    count = width // LANES
    recip = 1.0 / jnp.sum(got_ref[:, :count], axis=0)
    for i in range(count):
        recip_ref[:, i * LANES : (i + 1) * LANES] = recip[i : i + 1, :]

    def block(b, _):
        wait(b)
        at = pl.ds(pl.multiple_of(b * LANES, LANES), LANES)
        acc = jnp.zeros((LANES, LANES), jnp.float32)
        for j in range(width // LANES):
            lanes = slice(j * LANES, (j + 1) * LANES)
            acc += held_ref[at, lanes] * recip_ref[:, lanes]
        lines_ref[pl.ds(b, 1), :] = jnp.sum(jnp.transpose(acc), axis=0, keepdims=True)
        return 0

    lax.fori_loop(0, blocks, block, 0)
    for p in range(out_ref.shape[0]):
        out_ref[p, :8] = lines_ref[...]
        at = 8
        for ref in more:
            out_ref[p, at : at + ref.shape[0]] = ref[...]
            at += ref.shape[0]


def by_column_kernel(got_ref, e_ref, out_ref, lines_ref, acc_ref, held_ref, sem_ref):
    blocks, wait = fetch(e_ref, held_ref, sem_ref)
    width = e_ref.shape[1]
    lines_ref[...] = 1.0 / jnp.sum(got_ref[...], axis=0)
    acc_ref[...] = jnp.zeros_like(acc_ref)

    def block(b, _):
        wait(b)
        at = pl.ds(pl.multiple_of(b * LANES, LANES), LANES)
        scale = down(lines_ref[pl.ds(b, 1), :])
        for j in range(width // LANES):
            lanes = slice(j * LANES, (j + 1) * LANES)
            acc_ref[:, lanes] += fold(held_ref[at, lanes] * scale, 8)
        return 0

    lax.fori_loop(0, blocks, block, 0)
    to_all(acc_ref[...], out_ref, out_ref.shape[0])


def student_sums(s_ref, proto_ref, sums_ref):
    width = proto_ref.shape[1]

    def block(b, _):
        at = pl.ds(pl.multiple_of(b * 2 * LANES, 2 * LANES), 2 * LANES)
        acc = jnp.zeros((2 * LANES, LANES), jnp.float32)
        for j in range(width // 256):
            dots = jnp.dot(
                s_ref[at, :], proto_ref[:, j * 256 : (j + 1) * 256], preferred_element_type=jnp.float32
            )
            powers = jnp.exp2(dots * (LOG2E / TEMP_S))
            acc += powers[:, :LANES] + powers[:, LANES:]
        for i in range(2):
            part = acc[i * LANES : (i + 1) * LANES]
            sums_ref[pl.ds(b * 2 + i, 1), :] = jnp.sum(jnp.transpose(part), axis=0, keepdims=True)
        return 0

    lax.fori_loop(0, s_ref.shape[0] // (2 * LANES), block, 0)


def student_kernel(place_ref, s_ref, own_ref, other_ref, proto_ref, sums_ref):
    join_columns(place_ref, own_ref, other_ref, proto_ref, BY_BITS)
    student_sums(s_ref, proto_ref, sums_ref)


def slope_kernel(
    place_ref, lines_ref, recip_ref, s_ref, st_ref, ps_ref, psp_ref, e_ref,
    ug_ref, keep_ref, give_ref, slope_ref, total_ref, down_ref, here_ref, sem_ref,
):
    rows = st_ref.shape[2]
    width = ps_ref.shape[1]
    images = rows // CROPS
    tile = 1024
    g = pl.program_id(0)
    groups = pl.num_programs(0) - 1
    ordered = pltpu.make_async_copy(psp_ref, here_ref, sem_ref)

    @pl.when(g == 0)
    def _():
        total_ref[...] = jnp.zeros_like(total_ref)
        slope_ref[1] = jnp.zeros_like(slope_ref[1])
        ordered.start()

    def products(slot):
        total_ref[...] += jnp.dot(st_ref[0], slope_ref[slot], preferred_element_type=jnp.float32)
        unit = lax.dot_general(
            slope_ref[slot], ps_ref[...], (((1,), (1,)), ((), ())), preferred_element_type=jnp.float32
        )
        part = images // NY
        for crop in range(CROPS):
            for y in range(NY):
                ug_ref[0, y, crop * part : (crop + 1) * part, :] = unit[crop * images + y * part :][:part]

    def slopes_into(slot):
        for i in range(2):
            down_ref[i] = down(lines_ref[pl.ds(g * 2 + i, 1), :])
        for crop in range(CROPS):
            line = down(lines_ref[pl.ds(groups * 2 + g * CROPS + crop, 1), :])
            down_ref[2 + crop] = line if crop < 2 else 2.0 * line
        for j in range(width // tile):
            at = slice(j * tile, (j + 1) * tile)
            wide = lambda i: jnp.concatenate([down_ref[i]] * (tile // LANES), axis=1)
            recip = recip_ref[:, at]
            t0 = e_ref[:images, at] * recip * wide(0)
            t1 = e_ref[images:, at] * recip * wide(1)
            both = t0 + t1
            scores = jnp.dot(s_ref[0], ps_ref[:, at], preferred_element_type=jnp.float32)
            for crop in range(CROPS):
                lines = slice(crop * images, (crop + 1) * images)
                part = wide(2 + crop) * jnp.exp2(scores[lines] * (LOG2E / TEMP_S))
                minus = t1 if crop == 0 else t0 if crop == 1 else both
                slope_ref[slot, lines, at] = (part - minus).astype(jnp.bfloat16)

    for slot in range(2):

        @pl.when((g < groups) & (g % 2 == slot))
        def _():
            slopes_into(slot)
            products(1 - slot)

    @pl.when(g == groups)
    def _():
        products((NX - 1) % 2)

    @pl.when(g == groups)
    def _():
        ordered.wait()
        blocks = width // LANES
        part = total_ref.shape[0] // (NC * NZ)
        size = blocks * part
        for b in range(blocks):
            lanes = slice(b * LANES, (b + 1) * LANES)
            dot = jnp.sum(here_ref[:, lanes].astype(jnp.float32) * total_ref[:, lanes], axis=0, keepdims=True)
            keep_ref[NZ * size + b : NZ * size + b + 1, :] = dot
            give_ref[NZ * size + b : NZ * size + b + 1, :] = dot
        for side, ref in enumerate((keep_ref, give_ref)):
            half = lax.rem(place_ref[1] + side, NC) * NZ
            for k in range(NZ):
                z = lax.rem(place_ref[0] + k, NZ)
                lines = total_ref[pl.ds(pl.multiple_of((half + z) * part, part), part), :]
                for b in range(blocks):
                    at = k * size + b * part
                    ref[at : at + part, :] = lines[:, b * LANES : (b + 1) * LANES]


def local(teacher_feats, student_embeddings, teacher_weight, student_weight):
    images, _, bottleneck = teacher_feats.shape
    rows_here, wide = student_weight.shape
    sub = wide // (NX * NZ * NC)
    width = wide // NX
    total_k = wide * NY
    s_rows = images * CROPS
    t_rows = images * 2
    f32, bf16 = jnp.float32, jnp.bfloat16
    shape = jax.ShapeDtypeStruct
    place = jnp.stack([lax.axis_index("z"), lax.axis_index("core")]).astype(jnp.int32)
    exact = NX * t_rows * width

    t_float = teacher_feats.transpose(1, 0, 2).reshape(t_rows, bottleneck).astype(f32)
    t_unit = (t_float / jnp.sqrt(jnp.sum(t_float * t_float, axis=1, keepdims=True) + EPS)).astype(bf16)

    (shards,) = call(
        pack_kernel, [shape((NX * NZ * NC, 2 * rows_here, sub), f32)], [VMEM, VMEM], limit=58
    )(teacher_weight, student_weight)
    moved, t_unit = lax.optimization_barrier((swap(shards, DP), t_unit))
    t_all = along(t_unit, "x", NX).reshape(NX * t_rows, bottleneck)
    moved = moved.reshape(NX * NZ * NC, 2, rows_here, sub)
    cols_t = moved[:, 0].reshape(bottleneck, sub)
    cols_s = moved[:, 1].reshape(bottleneck, sub)
    col_t = jnp.sqrt(jnp.sum(cols_t * cols_t, axis=0) + EPS)
    col_s = jnp.sqrt(jnp.sum(cols_s * cols_s, axis=0) + EPS)
    mine_t = (cols_t / col_t).astype(bf16)
    mine_s = (cols_s / col_s).astype(bf16)

    s_raw = student_embeddings.transpose(1, 0, 2).reshape(s_rows, bottleneck).astype(f32)
    s_norm = jnp.sqrt(jnp.sum(s_raw * s_raw, axis=1, keepdims=True) + EPS)
    s_float = s_raw / s_norm
    s_unit, mine_t, mine_s = lax.optimization_barrier((s_float.astype(bf16), mine_t, mine_s))
    pair = exchanged(mine_s[None], "z", NZ, 4)
    s_pair = exchanged(s_unit[None], "x", NX, 1)
    own_t = spread(mine_t, "z", NZ)
    energy, to_devices = call(
        energy_kernel,
        [pltpu.HBM((NX * t_rows, width), f32), shape((NZ * NC, width // LANES + 8, LANES), f32)],
        [SMEM, VMEM, VMEM, VMEM, VMEM],
        [
            pltpu.VMEM((bottleneck, width), bf16),
            pltpu.VMEM((8, width), f32),
            pltpu.VMEM((NX * t_rows, width), f32),
            pltpu.SemaphoreType.DMA((width // 512,)),
        ],
        [HBM, VMEM],
        limit=24,
        flops=2 * exact * bottleneck,
        exps=exact,
    )(place, col_s.reshape(1, sub), t_all, own_t, other_core(own_t))

    energy = pltpu.with_memory_space_constraint(energy, pltpu.HBM)
    blocks = NX * t_rows // LANES
    held = [pltpu.VMEM((NX * t_rows, width), f32), pltpu.SemaphoreType.DMA((blocks,))]
    quarter = images // NY
    first = lax.axis_index("proto") * quarter
    part_float = lax.dynamic_slice_in_dim(s_float.reshape(CROPS, images, bottleneck), first, quarter, 1)
    part_norm = lax.dynamic_slice_in_dim(s_norm.reshape(CROPS, images, 1), first, quarter, 1)
    part_float, part_norm, to_devices = lax.optimization_barrier((part_float, part_norm, to_devices))

    def by_row(got, *more):
        lines = 8 + sum(m.shape[0] for m in more)
        return call(
            by_row_kernel,
            [shape((1, width), f32), shape((NX * NY, lines, LANES), f32)],
            [VMEM, HBM] + [VMEM] * len(more),
            [pltpu.VMEM((8, LANES), f32)] + held,
            limit=12,
            flops=2 * exact,
            moved=4 * exact,
        )(got, energy, *more)

    def by_column(got):
        (to_devices,) = call(
            by_column_kernel,
            [shape((NZ * NC, width // LANES, LANES), f32)],
            [VMEM, HBM],
            [pltpu.VMEM((8, LANES), f32), pltpu.VMEM((8, width), f32)] + held,
            limit=12,
            flops=2 * exact,
            moved=4 * exact,
        )(got, energy)
        return to_devices

    half_rows = NX * s_rows // 2
    student = dict(limit=20, flops=exact * 3 * bottleneck, exps=exact * 3 // 2)

    to_devices, own_s = lax.optimization_barrier((to_devices, merged(pair, "z", 4)))
    got = swap(to_devices, ZC)
    pair = exchanged(own_s, "z", NZ, 1)
    col_s = got[:, width // LANES].reshape(NZ, NC, LANES).transpose(1, 0, 2).reshape(NZ * NC, 1, LANES)
    _, to_devices = by_row(got)
    to_devices, own_s, s_all = lax.optimization_barrier((to_devices, merged(pair, "z", 1), merged(s_pair, "x", 1)))
    got = swap(to_devices, XY)
    pair = exchanged(own_s, "z", NZ, 2)
    to_devices = by_column(got)

    to_devices, own_s, s_all = lax.optimization_barrier((to_devices, merged(pair, "z", 2), s_all))
    got = swap(to_devices, ZC)
    other_s = other_core(own_s)
    s_pair = exchanged(s_all, "x", NX, 2)
    _, to_devices = by_row(got)
    to_devices, other_s, s_pair = lax.optimization_barrier((to_devices, other_s, s_pair))
    got = swap(to_devices, XY)
    s_all = merged(s_pair, "x", 2)
    s_halves = s_all.reshape(2, half_rows, bottleneck)
    proto_s, first_sums = call(
        student_kernel,
        [shape((bottleneck, width), bf16), shape((half_rows // LANES, LANES), f32)],
        [SMEM, VMEM, VMEM, VMEM],
        **student,
    )(place, s_halves[0], own_s, other_s)
    to_devices = by_column(got)

    to_devices, proto_s, s_all, first_sums = lax.optimization_barrier((to_devices, proto_s, s_all, first_sums))
    got = swap(to_devices, ZC)
    (last_sums,) = call(
        student_sums, [shape((half_rows // LANES, LANES), f32)], [VMEM, VMEM], **student
    )(s_all.reshape(2, half_rows, bottleneck)[1], proto_s)
    recip, to_devices = by_row(got, first_sums, last_sums)
    to_devices, proto_s, s_all = lax.optimization_barrier((to_devices, proto_s, s_all))
    got = swap(to_devices, XY)

    order = jnp.arange(bottleneck).reshape(NX, NZ, NC, rows_here).transpose(2, 1, 0, 3).reshape(-1)
    ordered = (order[:, None] == jnp.arange(bottleneck)[None, :]).astype(bf16)
    proto_o = jnp.dot(ordered, proto_s, preferred_element_type=f32).astype(bf16)
    s_o = jnp.einsum("pb,grb->gpr", ordered, s_all, preferred_element_type=f32).astype(bf16)
    size = bottleneck * width // (NC * NZ * LANES)
    unit_part, keep, give = call(
        slope_kernel,
        [pltpu.VMEM((NX, NY, s_rows // NY, bottleneck), f32)] + [pltpu.HBM((NZ * size + width // LANES, LANES), f32)] * NC,
        [
            SMEM,
            whole(NX * (2 + CROPS), LANES),
            whole(1, width),
            pl.BlockSpec((1, s_rows, bottleneck), lambda g: (jnp.minimum(g, NX - 1), 0, 0)),
            pl.BlockSpec((1, bottleneck, s_rows), lambda g: (jnp.maximum(g - 1, 0), 0, 0)),
            whole(bottleneck, width),
            HBM,
            pl.BlockSpec((t_rows, width), lambda g: (jnp.minimum(g, NX - 1), 0)),
        ],
        [
            pltpu.VMEM((2, s_rows, width), bf16),
            pltpu.VMEM((bottleneck, width), f32),
            pltpu.VMEM((2 + CROPS, LANES, LANES), f32),
            pltpu.VMEM((bottleneck, width), bf16),
            pltpu.SemaphoreType.DMA,
        ],
        [
            pl.BlockSpec((1, NY, s_rows // NY, bottleneck), lambda g: (jnp.maximum(g - 1, 0), 0, 0, 0)),
            whole(NZ * size + width // LANES, LANES),
            whole(NZ * size + width // LANES, LANES),
        ],
        (NX + 1,),
        limit=40,
        flops=6 * exact * 3 * bottleneck,
        moved=4 * exact,
        exps=exact * 3,
    )(
        place,
        total_k / 16.0 / jnp.sum(got, axis=0),
        recip,
        *(pltpu.with_memory_space_constraint(v, pltpu.HBM) for v in (s_all, s_o, proto_s, proto_o)),
        energy,
    )

    half = (keep + other_core(give)) * (1.0 / 512.0)
    dots = half[NZ * size :]
    high = lax.reduce_precision(dots, 5, 10)
    ends = [high.astype(jnp.float16), ((dots - high) * 1024.0).astype(jnp.float16)]
    proto_grad = half[:size]
    for k in range(1, NZ):
        sent = jnp.concatenate([half[k * size : (k + 1) * size].astype(jnp.float16)] + ends)
        came = shifted(sent, "z", NZ, k).astype(f32)
        proto_grad = proto_grad + came[:size]
        dots = dots + (came[size : size + NZ * NC] + came[size + NZ * NC :] * (1.0 / 1024.0))
    lines = bottleneck // (NC * NZ)
    proto_grad = proto_grad.reshape(NC * NZ, lines, LANES) * 512.0
    column_dot = dots.reshape(NC * NZ, 1, LANES) * 512.0
    at = (lax.axis_index("core") * NZ + lax.axis_index("z")) * lines
    proto_float = lax.dynamic_slice_in_dim(proto_o, at, lines, 0).astype(f32)
    proto_float = proto_float.reshape(lines, NC * NZ, LANES).transpose(1, 0, 2)
    grad_lines = (proto_grad - proto_float * column_dot) / col_s

    sent = (unit_part.reshape(NX * NY, CROPS * quarter, bottleneck) * 4.0).astype(jnp.float16)
    unit_grad = jnp.sum(swap(sent, XY).astype(f32), axis=0) * 0.25
    unit_grad = unit_grad.reshape(CROPS, quarter, bottleneck)
    fgrad = (unit_grad - part_float * jnp.sum(part_float * unit_grad, axis=2, keepdims=True)) / part_norm

    grad_lines, fgrad = lax.optimization_barrier((grad_lines, fgrad))
    feature_grad = along(fgrad.transpose(1, 0, 2), "proto", NY).reshape(images, CROPS, bottleneck)
    grad_lines = grad_lines.reshape(NC * NZ, NX, rows_here, LANES).transpose(1, 0, 2, 3)
    grad_rows = swap(grad_lines, "x").reshape(NX, NC, NZ, rows_here, LANES)
    weight_grad = grad_rows.transpose(3, 0, 2, 1, 4).reshape(rows_here, wide)
    teacher_new = 0.994 * teacher_weight + 0.006 * (student_weight - 0.5 * weight_grad)
    return weight_grad, teacher_new, feature_grad


def solution(mesh):
    fine = Mesh(mesh.devices.reshape(NX, NZ, NC, NY), ("x", "z", "core", "proto"))
    in_specs = (P(DP, None, None), P(DP, None, None), P(DP, "proto"), P(DP, "proto"))
    out_specs = (P(DP, "proto"), P(DP, "proto"), P(DP, None, None))
    return jax.shard_map(local, mesh=fine, in_specs=in_specs, out_specs=out_specs, check_vma=False)
```
